128 devices in a mesh: row: 8 (over y_hi, x), col: 16 (over y_lo, z, core).
Axes of the slice: x: 4, y: 4 (y_hi: 2, y_lo: 2; y = y_hi * 2 + y_lo), z: 4, core: 2. Of those that a mesh axis runs over, the one named last changes fastest.
Arguments:
- matrix: float32 [16384, 16384], P('row', 'col'), may hold values from -8 to 8, as said below
Outputs:
- next_matrix: float32 [16384, 16384], P('row', 'col')
The draws below stay inside these ranges and needn't reach their ends.
Inputs may be any that keep to these rules, and one draw needn't show every extreme that they name: matrix is symmetric; within each diagonal pair block (rows and columns 2 * 512 * p to 2 * 512 * (p + 1) - 1) any two diagonal entries differ by at least 4 / 512.
All inputs are finite; a program needn't handle non-finite values.
Results may differ from the reference program's by a relative error of at most 0.000098.
Values sent between devices are 32-bit elements; how exact they have to be, the bound alone decides.
No kernel may reach another device: no remote copies, remote signals or barrier semaphores. Data moves between devices by JAX's collectives and lax.ppermute only.
A program may use at most 128 MiB of HBM per device.

```python
import jax
import jax.numpy as jnp
import numpy as np
from jax import lax

B = 512
PAIRS = 16
ORDER = 16384


def draw_matrix(key, part):
    key = jax.random.fold_in(key, 11)
    key_off, key_perm, key_jitter = jax.random.split(key, 3)
    spacing = 8.0 / B
    off_scale = 0.1 * spacing
    noise_field = jax.random.normal(key_off, (ORDER, ORDER), jnp.float32)
    jitter = jax.random.uniform(key_jitter, (ORDER,), jnp.float32, -0.25, 0.25)
    symmetric = (noise_field + noise_field.T) * (off_scale * 0.70710678)
    pair_keys = jax.random.split(key_perm, PAIRS)
    rank_values = jax.vmap(lambda one_key: jax.random.permutation(one_key, 2 * B))(pair_keys)
    diagonal = spacing * (rank_values.reshape(ORDER).astype(jnp.float32) - (2 * B - 1) / 2.0 + jitter)
    row_ids = lax.broadcasted_iota(jnp.int32, (ORDER, ORDER), 0)
    col_ids = lax.broadcasted_iota(jnp.int32, (ORDER, ORDER), 1)
    return jnp.where(row_ids == col_ids, diagonal[:, None], symmetric)


def setup_inputs(seed: int = 0) -> dict:
    seeds = jax.random.split(jax.random.key(seed), 2)
    return {
        "matrix": draw_matrix(jax.random.fold_in(seeds[1], 71), 0),
    }


highest = lax.Precision.HIGHEST


def first_guess_of(pair_block):
    matrix_order = pair_block.shape[0]
    diagonal = jnp.diagonal(pair_block)
    spacing = diagonal[None, :] - diagonal[:, None]
    identity = jnp.eye(matrix_order, dtype=jnp.float32)
    correction = jnp.where(identity > 0, 0.0, pair_block / (spacing + identity))
    return identity + correction


def rotation_of(pair_block):
    first_guess = first_guess_of(pair_block)
    identity = jnp.eye(pair_block.shape[0], dtype=jnp.float32)
    correlation = jnp.dot(first_guess.T, first_guess, precision=highest, preferred_element_type=jnp.float32)
    return jnp.dot(first_guess, 1.5 * identity - 0.5 * correlation, precision=highest, preferred_element_type=jnp.float32)


def block_sources(slot_total):
    source_list = []
    for slot_index in range(slot_total):
        if slot_index == 0:
            source_list.append(0)
        elif slot_index == 1:
            source_list.append(1)
        else:
            source_list.append(2 * slot_index - 2)
        if slot_index < slot_total - 1:
            source_list.append(2 * slot_index + 3)
        else:
            source_list.append(2 * slot_index)
    return np.array(source_list, dtype=np.int32)


def reference(matrix):
    slot_total = PAIRS
    pair_width = 2 * B
    blocks = matrix.reshape(slot_total, pair_width, slot_total, pair_width)
    pair_blocks = jnp.stack([blocks[slot_index, :, slot_index, :] for slot_index in range(slot_total)])
    rotations = lax.map(rotation_of, pair_blocks)
    left_done = jnp.einsum("pji,pjn->pin", rotations, matrix.reshape(slot_total, pair_width, ORDER), precision=highest)
    rotated = jnp.einsum("mpj,pjk->mpk", left_done.reshape(ORDER, slot_total, pair_width), rotations, precision=highest)
    source = block_sources(slot_total)
    tile_grid = rotated.reshape(2 * slot_total, B, 2 * slot_total, B)
    moved_rows = jnp.take(tile_grid, source, axis=0)
    moved_both = jnp.take(moved_rows, source, axis=2)
    return moved_both.reshape(ORDER, ORDER)
```

```python
import functools

import jax
import jax.numpy as jnp
from jax import lax
from jax.experimental import pallas as pl
from jax.experimental.pallas import tpu as pltpu
from jax.sharding import PartitionSpec as P

f32, bf16, i32 = jnp.float32, jnp.bfloat16, jnp.int32
AXES = ("row", "col")
VMEM_LIMIT = 56 * 1024 * 1024


def cost(flops, nbytes):
    return pl.CostEstimate(flops=flops, bytes_accessed=nbytes, transcendentals=0)


def split(value):
    high = value.astype(bf16)
    return high, (value - high.astype(f32)).astype(bf16)


def dot(a, b):
    return jnp.dot(a, b, preferred_element_type=f32)


def dot3(a_high, a_low, b_high, b_low):
    return dot(a_high, b_high) + (dot(a_high, b_low) + dot(a_low, b_high))


def pack_kernel(info_ref, block_ref, packed_ref):
    width = block_ref.shape[0]
    half = width // 2
    rows = lax.broadcasted_iota(i32, (half, half), 0)
    cols = lax.broadcasted_iota(i32, (half, half), 1)
    on_diagonal = rows == cols
    top = block_ref[:half, :half]
    bottom = block_ref[half:, half:]
    top_only = jnp.where(on_diagonal, top, 0.0)
    bottom_only = jnp.where(on_diagonal, bottom, 0.0)
    top_down = jnp.sum(top_only, axis=1, keepdims=True)
    top_across = jnp.sum(top_only, axis=0, keepdims=True)
    bottom_down = jnp.sum(bottom_only, axis=1, keepdims=True)
    bottom_across = jnp.sum(bottom_only, axis=0, keepdims=True)
    above = rows < cols
    value = jnp.where(above, top, bottom)
    spacing = jnp.where(above, top_across - top_down, bottom_across - bottom_down)
    packed_ref[:, :half] = jnp.where(
        on_diagonal, 0.0, value / jnp.where(on_diagonal, 1.0, spacing)
    )
    packed_ref[:, half:] = block_ref[:half, half:] / (bottom_across - top_down)


def pack(info, matrix):
    width = matrix.shape[1]
    half = width // 2
    return pl.pallas_call(
        pack_kernel,
        out_shape=jax.ShapeDtypeStruct((half, width), f32),
        grid_spec=pltpu.PrefetchScalarGridSpec(
            num_scalar_prefetch=1,
            grid=(1,),
            in_specs=[pl.BlockSpec((width, width), lambda i, info: (info[0], 0))],
            out_specs=pl.BlockSpec((half, width), lambda i, info: (0, 0)),
        ),
        compiler_params=pltpu.CompilerParams(vmem_limit_bytes=VMEM_LIMIT),
        cost_estimate=cost(8 * width * width, 6 * width * width),
        name="pack",
    )(info, matrix)


def rotation_kernel(sign, place_ref, *refs):
    count = 8
    pieces = refs[:count]
    outs = refs[count:-5]
    packed, e_high, e_low, t_high, t_low = refs[-5:]
    depth, width = pieces[0].shape
    half = width // 2
    for k in range(count):
        packed[pl.ds(pl.multiple_of(place_ref[k] * depth, depth), depth), :] = pieces[k][...]
    rows = lax.broadcasted_iota(i32, (half, half), 0)
    cols = lax.broadcasted_iota(i32, (half, half), 1)
    triangles = packed[:, :half]
    flipped = -triangles.T
    corner = packed[:, half:]

    def put(r, c, value):
        if sign < 0:
            value = -value
        high, low = split(value)
        e_high[r * half : (r + 1) * half, c * half : (c + 1) * half] = high
        e_low[r * half : (r + 1) * half, c * half : (c + 1) * half] = low

    put(0, 0, jnp.where(rows < cols, triangles, flipped))
    put(1, 1, jnp.where(rows > cols, triangles, flipped))
    put(0, 1, corner)
    put(1, 0, -corner.T)
    tile = 256

    @pl.loop(0, width // tile)
    def _(n):
        at = pl.ds(pl.multiple_of(n * tile, tile), tile)
        square = dot3(e_high[...], e_low[...], e_high[:, at], e_low[:, at])
        high, low = split(0.5 * square)
        t_high[:, at] = high
        t_low[:, at] = low

    @pl.loop(0, width // tile)
    def _(n):
        at = pl.ds(pl.multiple_of(n * tile, tile), tile)
        cube = dot3(e_high[...], e_low[...], t_high[:, at], t_low[:, at])
        here = lax.broadcasted_iota(i32, (width, tile), 0)
        there = lax.broadcasted_iota(i32, (width, tile), 1) + n * tile
        total = cube + (t_high[:, at].astype(f32) + t_low[:, at].astype(f32))
        total = total + (e_high[:, at].astype(f32) + e_low[:, at].astype(f32))
        total = total + jnp.where(here == there, 1.0, 0.0)
        if len(outs) == 1:
            outs[0][:, at] = total
        else:
            high, low = split(total)
            outs[0][:, at] = high
            outs[1][:, at] = low


def rotation(place, pieces, sign, in_parts, name):
    depth, width = pieces[0].shape
    square = (width, width)
    if in_parts:
        shapes = [jax.ShapeDtypeStruct(square, bf16)] * 2
    else:
        shapes = [jax.ShapeDtypeStruct(square, f32)]
    return pl.pallas_call(
        functools.partial(rotation_kernel, sign),
        out_shape=shapes,
        in_specs=[pl.BlockSpec(memory_space=pltpu.SMEM)]
        + [pl.BlockSpec(memory_space=pltpu.VMEM)] * len(pieces),
        out_specs=[pl.BlockSpec(memory_space=pltpu.VMEM)] * len(shapes),
        scratch_shapes=[pltpu.VMEM((width // 2, width), f32)] + [pltpu.VMEM(square, bf16)] * 4,
        compiler_params=pltpu.CompilerParams(vmem_limit_bytes=VMEM_LIMIT),
        cost_estimate=cost(12 * width**3, 6 * width * width),
        name=name,
    )(place, *pieces)


def right_kernel(info_ref, m_ref, high_ref, low_ref, out_ref):
    m_high, m_low = split(m_ref[...])
    out_ref[...] = dot3(m_high, m_low, high_ref[...], low_ref[...])


def right(info, matrix, r_high, r_low, name):
    width = matrix.shape[1]
    half = width // 2
    tile = 256
    per_slot = width // tile
    return pl.pallas_call(
        right_kernel,
        out_shape=jax.ShapeDtypeStruct((width, half), f32),
        grid_spec=pltpu.PrefetchScalarGridSpec(
            num_scalar_prefetch=1,
            grid=(per_slot,),
            in_specs=[
                pl.BlockSpec((tile, width), lambda i, info: (info[0] * per_slot + i, 0)),
                pl.BlockSpec((width, half), lambda i, info: (0, info[1])),
                pl.BlockSpec((width, half), lambda i, info: (0, info[1])),
            ],
            out_specs=pl.BlockSpec((tile, half), lambda i, info: (i, 0)),
        ),
        compiler_params=pltpu.CompilerParams(vmem_limit_bytes=VMEM_LIMIT),
        cost_estimate=cost(3 * width**3, 8 * width * width),
        name=name,
    )(info, matrix, r_high, r_low)


def left_kernel(info_ref, *refs):
    turned_ref, part_ref = refs[:2]
    moved_ref, kept_ref, part_high, part_low = refs[-4:]
    step = pl.program_id(0)
    steps = pl.num_programs(0)

    @pl.when(step == 0)
    def _():
        high, low = split(part_ref[...])
        part_high[...] = high
        part_low[...] = low

    t_high, t_low = split(turned_ref[...])
    value = dot3(t_high, t_low, part_high[...], part_low[...])

    @pl.when(step < steps // 2)
    def _():
        moved_ref[...] = value

    @pl.when(step >= steps // 2)
    def _():
        kept_ref[...] = value


def left(info, turned, part, result, out_rows, name):
    width = turned.shape[0]
    half = width // 2
    tile = 256
    per_half = half // tile
    out_shape = jax.ShapeDtypeStruct((out_rows, width), f32)

    def row_tile(i, info):
        which = jnp.where(i < per_half, info[0], 1 - info[0])
        return (which * per_half + lax.rem(i, per_half), 0)

    operands = [turned, part]
    in_specs = [
        pl.BlockSpec((tile, width), row_tile),
        pl.BlockSpec((width, half), lambda i, info: (0, 0)),
    ]
    aliases = {}
    if result is not None:
        operands.append(result)
        in_specs.append(pl.BlockSpec(memory_space=pl.ANY))
        aliases = {3: 1}
    return pl.pallas_call(
        left_kernel,
        out_shape=[jax.ShapeDtypeStruct((half, half), f32), out_shape],
        grid_spec=pltpu.PrefetchScalarGridSpec(
            num_scalar_prefetch=1,
            grid=(2 * per_half,),
            in_specs=in_specs,
            out_specs=[
                pl.BlockSpec((tile, half), lambda i, info: (jnp.minimum(i, per_half - 1), 0)),
                pl.BlockSpec(
                    (tile, half),
                    lambda i, info: (info[1] * per_half + jnp.maximum(i - per_half, 0), info[2]),
                ),
            ],
            scratch_shapes=[pltpu.VMEM((width, half), bf16)] * 2,
        ),
        input_output_aliases=aliases,
        compiler_params=pltpu.CompilerParams(vmem_limit_bytes=VMEM_LIMIT),
        cost_estimate=cost(3 * width**3, 10 * width * width),
        name=name,
    )(info, *operands)


def land_kernel(info_ref, arrived_ref, own_ref, result_ref, out_ref):
    out_ref[...] = jnp.where(info_ref[2] > 0, own_ref[...], arrived_ref[...])


def land(info, arrived, own, result, name):
    half = arrived.shape[0]
    tile = 256
    per_half = half // tile
    part = pl.BlockSpec((tile, half), lambda i, info: (i, 0))
    return pl.pallas_call(
        land_kernel,
        out_shape=jax.ShapeDtypeStruct(result.shape, f32),
        grid_spec=pltpu.PrefetchScalarGridSpec(
            num_scalar_prefetch=1,
            grid=(per_half,),
            in_specs=[part, part, pl.BlockSpec(memory_space=pl.ANY)],
            out_specs=pl.BlockSpec(
                (tile, half), lambda i, info: (info[0] * per_half + i, info[1])
            ),
        ),
        input_output_aliases={3: 0},
        compiler_params=pltpu.CompilerParams(vmem_limit_bytes=VMEM_LIMIT),
        cost_estimate=cost(half * half, 12 * half * half),
        name=name,
    )(info, arrived, own, result)


OFFSETS = [(1, 0), (3, 0), (2, 0), (0, 1), (1, 1), (3, 1), (2, 1)]


def shifted(member, offset):
    ring, plane = offset
    return (member // 4 ^ plane) * 4 + (member + ring) % 4


def group_pairs(group, offset, only_source):
    pairs = []
    for row in range(8):
        for col in range(16):
            chip, core = col // 2, col % 2
            if only_source and row != chip:
                continue
            if group == "row":
                target = (shifted(row, offset), col)
            else:
                target = (row, 2 * shifted(chip, offset) + core)
            pairs.append((row * 16 + col, target[0] * 16 + target[1]))
    return pairs


def spread(packed, group, member, is_source):
    depth = packed.shape[0] // 8

    def piece(at):
        return lax.dynamic_slice_in_dim(packed, at * depth, depth, 0)

    arrived = [
        lax.ppermute(piece(shifted(member, offset)), AXES, group_pairs(group, offset, True))
        for offset in OFFSETS
    ]
    own = jnp.where(is_source, piece(member), sum(arrived[1:], arrived[0]))
    pieces = [own]
    places = [member]
    for ring, plane in OFFSETS:
        pieces.append(lax.ppermute(own, AXES, group_pairs(group, (ring, plane), False)))
        places.append(shifted(member, (4 - ring, plane)))
    return pieces, jnp.stack(places).astype(i32)


def local(matrix):
    row = lax.axis_index("row")
    col = lax.axis_index("col")
    chip = col // 2
    core = col % 2
    is_source = row == chip
    rows_here = matrix.shape[0]

    def scalars(*values):
        return jnp.stack([jnp.asarray(v, i32) for v in values])

    packed = pack(scalars(core), matrix)
    col_pieces, col_places = spread(packed, "row", row, is_source)
    row_pieces, row_places = spread(packed, "col", chip, is_source)

    r_high, r_low = rotation(col_places, col_pieces, 1, True, "column_rotation")
    near_half = jnp.where((core == 1) | (col == 0), 1, 0)
    swap = [(i, i ^ 1) for i in range(16)]
    chips = [(0, 0), (15, 15)]
    chips += [(i, i - 1) for i in range(2, 16, 2)] + [(i, i + 1) for i in range(1, 15, 2)]
    first, second = 1 - core, core
    at_end = (col == 0) | (col == 15)
    end_first, end_second = jnp.where(at_end, core, first), jnp.where(at_end, first, core)
    far_first = right(scalars(end_first, 1 - near_half), matrix, r_high, r_low, "right_far_first")
    far_first = lax.ppermute(far_first, "col", chips)
    near_first = right(scalars(first, near_half), matrix, r_high, r_low, "right_near_first")
    near_first = lax.ppermute(near_first, "col", swap)
    near_second = right(scalars(second, near_half), matrix, r_high, r_low, "right_near_second")
    near_second = lax.ppermute(near_second, "col", swap)
    far_second = right(scalars(end_second, 1 - near_half), matrix, r_high, r_low, "right_far_second")
    far_second = lax.ppermute(far_second, "col", chips)

    (turned,) = rotation(row_places, row_pieces, -1, False, "row_rotation")
    other_turned = lax.ppermute(turned, "col", swap)

    def out_half(slot):
        return jnp.where(slot == 0, jnp.where(row == 0, 0, 1), 0)

    near_block, far_block = 1 - core, core
    kept_row_first = jnp.where(core == 0, 2, 1)
    kept_row_second = jnp.where(core == 0, 1, 2)
    land_row_first = jnp.where(core == 0, 3, 0)
    land_row_second = jnp.where(core == 0, 0, 3)
    end_first = jnp.where(core == 0, row == 7, row == 0)
    end_second = jnp.where(core == 0, row == 0, row == 7)

    def row_pairs(down_core):
        pairs = []
        for r in range(8):
            for c in range(16):
                target = r - 1 if c % 2 == down_core else r + 1
                if 0 <= target < 8:
                    pairs.append((r * 16 + c, target * 16 + c))
        return pairs

    result = None
    parts = {}
    for place, part, block in (
        ("near", (near_first, near_second), near_block),
        ("far", (far_first, far_second), far_block),
    ):
        for order in range(2):
            slot = (core, 1 - core)[order]
            kept_row = (kept_row_first, kept_row_second)[order]
            moved, result = left(
                scalars(out_half(slot), kept_row, block),
                (turned, other_turned)[order],
                part[order],
                result,
                rows_here,
                "left_%s_%d" % (place, order),
            )
            arrived = lax.ppermute(moved, AXES, row_pairs(order))
            parts[place, order] = moved, arrived
    for place, block in (("near", near_block), ("far", far_block)):
        for order in range(2):
            end = (end_first, end_second)[order]
            land_row = (land_row_first, land_row_second)[order]
            result = land(
                scalars(land_row, block, end),
                parts[place, order][1],
                parts[place, 1 - order][0],
                result,
                "land_%s_%d" % (place, order),
            )
    return result


def solution(mesh):
    return jax.shard_map(
        local, mesh=mesh, in_specs=(P("row", "col"),), out_specs=P("row", "col"), check_vma=False
    )
```

```python
import functools

import jax
import jax.numpy as jnp
from jax import lax
from jax.experimental import pallas as pl
from jax.experimental.pallas import tpu as pltpu
from jax.sharding import PartitionSpec as P

f32, bf16, i32 = jnp.float32, jnp.bfloat16, jnp.int32
AXES = ("row", "col")
VMEM_LIMIT = 56 * 1024 * 1024


def cost(flops, nbytes):
    return pl.CostEstimate(flops=flops, bytes_accessed=nbytes, transcendentals=0)


def split(value):
    high = value.astype(bf16)
    return high, (value - high.astype(f32)).astype(bf16)


def dot(a, b):
    return jnp.dot(a, b, preferred_element_type=f32)


def dot3(a_high, a_low, b_high, b_low):
    return dot(a_high, b_high) + (dot(a_high, b_low) + dot(a_low, b_high))


CORE, SOURCE, FAR_FIRST, FAR_SECOND, FAR_HALF, NEAR_HALF, NEAR_FIRST, NEAR_SECOND = range(8)
OUT_FIRST, OUT_SECOND, KEPT_FIRST, KEPT_SECOND, NEAR_BLOCK, FAR_BLOCK = range(8, 14)
LAND_FIRST, LAND_SECOND, END_FIRST, END_SECOND = range(14, 18)
PLACES = 18


def pack_kernel(info_ref, block_ref, packed_ref, masked_ref):
    width = block_ref.shape[0]
    half = width // 2
    rows = lax.broadcasted_iota(i32, (half, half), 0)
    cols = lax.broadcasted_iota(i32, (half, half), 1)
    on_diagonal = rows == cols
    top = block_ref[:half, :half]
    bottom = block_ref[half:, half:]
    top_only = jnp.where(on_diagonal, top, 0.0)
    bottom_only = jnp.where(on_diagonal, bottom, 0.0)
    top_down = jnp.sum(top_only, axis=1, keepdims=True)
    top_across = jnp.sum(top_only, axis=0, keepdims=True)
    bottom_down = jnp.sum(bottom_only, axis=1, keepdims=True)
    bottom_across = jnp.sum(bottom_only, axis=0, keepdims=True)
    above = rows < cols
    value = jnp.where(above, top, bottom)
    spacing = jnp.where(above, top_across - top_down, bottom_across - bottom_down)
    triangles = jnp.where(on_diagonal, 0.0, value / jnp.where(on_diagonal, 1.0, spacing))
    corner = block_ref[:half, half:] / (bottom_across - top_down)
    here = info_ref[SOURCE] > 0
    packed_ref[:, :half] = triangles
    packed_ref[:, half:] = corner
    masked_ref[:, :half] = jnp.where(here, triangles, 0.0)
    masked_ref[:, half:] = jnp.where(here, corner, 0.0)


def pack(info, matrix):
    width = matrix.shape[1]
    half = width // 2
    out = jax.ShapeDtypeStruct((half, width), f32)
    out_spec = pl.BlockSpec((half, width), lambda i, info: (0, 0))
    return pl.pallas_call(
        pack_kernel,
        out_shape=[out, out],
        grid_spec=pltpu.PrefetchScalarGridSpec(
            num_scalar_prefetch=1,
            grid=(1,),
            in_specs=[pl.BlockSpec((width, width), lambda i, info: (info[CORE], 0))],
            out_specs=[out_spec, out_spec],
        ),
        compiler_params=pltpu.CompilerParams(vmem_limit_bytes=VMEM_LIMIT),
        cost_estimate=cost(8 * width * width, 8 * width * width),
        name="pack",
    )(info, matrix)


def rotation_kernel(sign, count, in_parts, info_ref, *refs):
    pieces = refs[:count]
    outs = refs[-7:-5] if in_parts else refs[-6:-5]
    packed, e_high, e_low, t_high, t_low = refs[-5:]
    depth, width = pieces[0].shape
    half = width // 2
    if count == 1:
        packed = pieces[0]
    else:
        for k in range(count):
            at = pl.multiple_of(info_ref[PLACES + k] * depth, depth)
            packed[pl.ds(at, depth), :] = pieces[k][...]
    rows = lax.broadcasted_iota(i32, (half, half), 0)
    cols = lax.broadcasted_iota(i32, (half, half), 1)
    triangles = packed[:, :half]
    flipped = -triangles.T
    corner = packed[:, half:]

    def put(r, c, value):
        if sign < 0:
            value = -value
        high, low = split(value)
        e_high[r * half : (r + 1) * half, c * half : (c + 1) * half] = high
        e_low[r * half : (r + 1) * half, c * half : (c + 1) * half] = low

    put(0, 0, jnp.where(rows < cols, triangles, flipped))
    put(1, 1, jnp.where(rows > cols, triangles, flipped))
    put(0, 1, corner)
    put(1, 0, -corner.T)
    tile = 256

    for n in range(width // tile):
        lo, hi = n * tile, (n + 1) * tile
        square = 0.5 * dot3(e_high[:hi, :], e_low[:hi, :], e_high[:, lo:hi], e_low[:, lo:hi])
        t_high[:hi, lo:hi], t_low[:hi, lo:hi] = split(square)
        if n > 0:
            t_high[lo:hi, :lo], t_low[lo:hi, :lo] = split(square[:lo].T)

    def store(r0, r1, c0, c1, value):
        if in_parts:
            outs[0][r0:r1, c0:c1], outs[1][r0:r1, c0:c1] = split(value)
        else:
            outs[0][r0:r1, c0:c1] = value

    for n in range(width // tile):
        lo, hi = n * tile, (n + 1) * tile
        odd = dot3(e_high[:hi, :], e_low[:hi, :], t_high[:, lo:hi], t_low[:, lo:hi])
        odd = odd + (e_high[:hi, lo:hi].astype(f32) + e_low[:hi, lo:hi].astype(f32))
        even = t_high[:hi, lo:hi].astype(f32) + t_low[:hi, lo:hi].astype(f32)
        here = lax.broadcasted_iota(i32, (hi, tile), 0)
        there = lax.broadcasted_iota(i32, (hi, tile), 1) + lo
        store(0, hi, lo, hi, even + odd + jnp.where(here == there, 1.0, 0.0))
        if n > 0:
            store(lo, hi, 0, lo, (even[:lo] - odd[:lo]).T)


def rotation(info, pieces, sign, in_parts, after, name):
    depth, width = pieces[0].shape
    square = (width, width)
    if in_parts:
        shapes = [jax.ShapeDtypeStruct(square, bf16)] * 2
    else:
        shapes = [jax.ShapeDtypeStruct(square, f32)]
    return pl.pallas_call(
        functools.partial(rotation_kernel, sign, len(pieces), in_parts),
        out_shape=shapes,
        in_specs=[pl.BlockSpec(memory_space=pltpu.SMEM)]
        + [pl.BlockSpec(memory_space=pltpu.VMEM)] * len(pieces)
        + [pl.BlockSpec(memory_space=pl.ANY)] * len(after),
        out_specs=[pl.BlockSpec(memory_space=pltpu.VMEM)] * len(shapes),
        scratch_shapes=[pltpu.VMEM((width // 2, width), f32)] + [pltpu.VMEM(square, bf16)] * 4,
        compiler_params=pltpu.CompilerParams(vmem_limit_bytes=VMEM_LIMIT),
        cost_estimate=cost(12 * width**3, 6 * width * width),
        name=name,
    )(info, *pieces, *after)


def right_kernel(info_ref, m_ref, high_ref, low_ref, *refs):
    m_high, m_low = split(m_ref[...])
    refs[-1][...] = dot3(m_high, m_low, high_ref[...], low_ref[...])


def right(info, slots, which, matrix, r_high, r_low, after, name):
    width = matrix.shape[1]
    half = width // 2
    tile = 512
    per_slot = width // tile

    def from_matrix(i, info):
        slot = info[slots[0]]
        if len(slots) > 1:
            slot = jnp.where(i < per_slot, slot, info[slots[1]])
        return (slot * per_slot + lax.rem(i, per_slot), 0)

    return pl.pallas_call(
        right_kernel,
        out_shape=jax.ShapeDtypeStruct((len(slots) * width, half), f32),
        grid_spec=pltpu.PrefetchScalarGridSpec(
            num_scalar_prefetch=1,
            grid=(per_slot * len(slots),),
            in_specs=[
                pl.BlockSpec((tile, width), from_matrix),
                pl.BlockSpec((width, half), lambda i, info: (0, info[which])),
                pl.BlockSpec((width, half), lambda i, info: (0, info[which])),
            ]
            + [pl.BlockSpec(memory_space=pl.ANY)] * len(after),
            out_specs=pl.BlockSpec((tile, half), lambda i, info: (i, 0)),
        ),
        compiler_params=pltpu.CompilerParams(vmem_limit_bytes=VMEM_LIMIT),
        cost_estimate=cost(3 * len(slots) * width**3, 8 * width * width),
        name=name,
    )(info, matrix, r_high, r_low, *after)


def left_kernel(info_ref, *refs):
    turned_ref, part_ref = refs[:2]
    moved_ref, kept_ref, part_high, part_low = refs[-4:]
    step = pl.program_id(0)

    @pl.when(step == 0)
    def _():
        part_high[...], part_low[...] = split(part_ref[...])

    t_high, t_low = split(turned_ref[...])
    value = dot3(t_high, t_low, part_high[...], part_low[...])

    @pl.when(step == 0)
    def _():
        moved_ref[...] = value

    @pl.when(step == 1)
    def _():
        kept_ref[...] = value


def left(info, out_half, kept_row, block, turned, part, part_at, result, out_rows, name):
    width = turned.shape[0]
    half = width // 2
    operands = [turned, part]
    in_specs = [
        pl.BlockSpec(
            (half, width), lambda i, info: (jnp.where(i == 0, info[out_half], 1 - info[out_half]), 0)
        ),
        pl.BlockSpec((width, half), lambda i, info: (part_at, 0)),
    ]
    aliases = {}
    if result is not None:
        operands.append(result)
        in_specs.append(pl.BlockSpec(memory_space=pl.ANY))
        aliases = {3: 1}
    return pl.pallas_call(
        left_kernel,
        out_shape=[
            jax.ShapeDtypeStruct((half, half), f32),
            jax.ShapeDtypeStruct((out_rows, width), f32),
        ],
        grid_spec=pltpu.PrefetchScalarGridSpec(
            num_scalar_prefetch=1,
            grid=(2,),
            in_specs=in_specs,
            out_specs=[
                pl.BlockSpec((half, half), lambda i, info: (0, 0)),
                pl.BlockSpec((half, half), lambda i, info: (info[kept_row], info[block])),
            ],
            scratch_shapes=[pltpu.VMEM((width, half), bf16)] * 2,
        ),
        input_output_aliases=aliases,
        compiler_params=pltpu.CompilerParams(vmem_limit_bytes=VMEM_LIMIT),
        cost_estimate=cost(3 * width**3, 10 * width * width),
        name=name,
    )(info, *operands)


def land_kernel(parts, info_ref, *refs):
    count = len(parts)
    out_ref, sems = refs[-2:]
    half = refs[0].shape[0]

    def copy(k, source):
        row, block, _ = parts[k]
        rows = pl.ds(pl.multiple_of(info_ref[row] * half, half), half)
        cols = pl.ds(pl.multiple_of(info_ref[block] * half, half), half)
        return pltpu.make_async_copy(source, out_ref.at[rows, cols], sems.at[k])

    for k in range(count):
        own = info_ref[parts[k][2]] > 0

        @pl.when(own)
        def _():
            copy(k, refs[count + k]).start()

        @pl.when(jnp.logical_not(own))
        def _():
            copy(k, refs[k]).start()

    for k in range(count):
        copy(k, refs[k]).wait()


def land(info, parts, arrived, own, result, name):
    half = arrived[0].shape[0]
    anywhere = pl.BlockSpec(memory_space=pl.ANY)
    count = len(parts)
    return pl.pallas_call(
        functools.partial(land_kernel, parts),
        out_shape=jax.ShapeDtypeStruct(result.shape, f32),
        in_specs=[pl.BlockSpec(memory_space=pltpu.SMEM)] + [anywhere] * (2 * count + 1),
        out_specs=anywhere,
        scratch_shapes=[pltpu.SemaphoreType.DMA((count,))],
        input_output_aliases={2 * count + 1: 0},
        compiler_params=pltpu.CompilerParams(vmem_limit_bytes=VMEM_LIMIT),
        cost_estimate=cost(half * half, 8 * count * half * half),
        name=name,
    )(info, *arrived, *own, result)


OFFSETS = [(1, 0), (3, 0), (2, 0), (0, 1), (1, 1), (3, 1), (2, 1)]


def shifted(member, offset):
    ring, plane = offset
    return (member // 4 ^ plane) * 4 + (member + ring) % 4


def group_pairs(group, offset, only_source):
    pairs = []
    for row in range(8):
        for col in range(16):
            chip, core = col // 2, col % 2
            if only_source and row != chip:
                continue
            if group == "row":
                target = (shifted(row, offset), col)
            else:
                target = (row, 2 * shifted(chip, offset) + core)
            pairs.append((row * 16 + col, target[0] * 16 + target[1]))
    return pairs


def spread(packed, group, member, is_source):
    depth = packed.shape[0] // 8

    def piece(at):
        return lax.dynamic_slice_in_dim(packed, at * depth, depth, 0)

    arrived = [
        lax.ppermute(piece(shifted(member, offset)), AXES, group_pairs(group, offset, True))
        for offset in OFFSETS
    ]
    own = jnp.where(is_source, piece(member), sum(arrived[1:], arrived[0]))
    return [own] + [
        lax.ppermute(own, AXES, group_pairs(group, offset, False)) for offset in OFFSETS
    ]


def local(matrix):
    row = lax.axis_index("row")
    col = lax.axis_index("col")
    chip = col // 2
    core = col % 2
    is_source = row == chip
    rows_here = matrix.shape[0]
    at_end = (col == 0) | (col == 15)
    near_half = jnp.where((core == 1) | (col == 0), 1, 0)
    out_top = jnp.where(row == 0, 0, 1)
    values = {
        CORE: core,
        SOURCE: is_source,
        FAR_FIRST: jnp.where(at_end, core, 1 - core),
        FAR_SECOND: jnp.where(at_end, 1 - core, core),
        FAR_HALF: 1 - near_half,
        NEAR_HALF: near_half,
        NEAR_FIRST: 1 - core,
        NEAR_SECOND: core,
        OUT_FIRST: jnp.where(core == 0, out_top, 0),
        OUT_SECOND: jnp.where(core == 0, 0, out_top),
        KEPT_FIRST: jnp.where(core == 0, 2, 1),
        KEPT_SECOND: jnp.where(core == 0, 1, 2),
        NEAR_BLOCK: 1 - core,
        FAR_BLOCK: core,
        LAND_FIRST: jnp.where(core == 0, 3, 0),
        LAND_SECOND: jnp.where(core == 0, 0, 3),
        END_FIRST: jnp.where(core == 0, row == 7, row == 0),
        END_SECOND: jnp.where(core == 0, row == 0, row == 7),
        PLACES: row,
    }
    for k, (ring, plane) in enumerate(OFFSETS):
        values[PLACES + 1 + k] = shifted(row, (4 - ring, plane))
    info = jnp.stack([jnp.asarray(values[k], i32) for k in range(len(values))])

    packed, masked = pack(info, matrix)
    alike = [list(range(0, 16, 2)), list(range(1, 16, 2))]
    row_packed = lax.psum(masked, "col", axis_index_groups=alike)
    col_pieces = spread(packed, "row", row, is_source)

    r_high, r_low = rotation(info, col_pieces, 1, True, [], "column_rotation")
    swap = [(i, i ^ 1) for i in range(16)]
    chips = [(0, 0), (15, 15)]
    chips += [(i, i - 1) for i in range(2, 16, 2)] + [(i, i + 1) for i in range(1, 15, 2)]
    to_send = right(
        info, [FAR_FIRST], FAR_HALF, matrix, r_high, r_low, [], "right_far_first"
    )
    far_first = lax.ppermute(to_send, "col", chips)
    to_send = right(
        info, [NEAR_FIRST, NEAR_SECOND], NEAR_HALF, matrix, r_high, r_low, [to_send], "right_near"
    )
    near = lax.ppermute(to_send, "col", swap)
    to_send = right(
        info, [FAR_SECOND], FAR_HALF, matrix, r_high, r_low, [to_send], "right_far_second"
    )
    far_second = lax.ppermute(to_send, "col", chips)

    (turned,) = rotation(info, [row_packed], -1, False, [to_send], "row_rotation")
    other_turned = lax.ppermute(turned, "col", swap)

    def row_pairs(down_core):
        pairs = []
        for r in range(8):
            for c in range(16):
                target = r - 1 if c % 2 == down_core else r + 1
                if 0 <= target < 8:
                    pairs.append((r * 16 + c, target * 16 + c))
        return pairs

    result = None
    moved, arrived = [], []
    for name, order, block, part, part_at in (
        ("left_near_first", 0, NEAR_BLOCK, near, 0),
        ("left_far_first", 0, FAR_BLOCK, far_first, 0),
        ("left_near_second", 1, NEAR_BLOCK, near, 1),
        ("left_far_second", 1, FAR_BLOCK, far_second, 0),
    ):
        leaving, result = left(
            info,
            (OUT_FIRST, OUT_SECOND)[order],
            (KEPT_FIRST, KEPT_SECOND)[order],
            block,
            (turned, other_turned)[order],
            part,
            part_at,
            result,
            rows_here,
            name,
        )
        moved.append(leaving)
        arrived.append(lax.ppermute(leaving, AXES, row_pairs(order)))
    first, second = (LAND_FIRST, END_FIRST), (LAND_SECOND, END_SECOND)
    parts = [
        (order[0], block, order[1])
        for order in (first, second)
        for block in (NEAR_BLOCK, FAR_BLOCK)
    ]
    own = moved[2:] + moved[:2]
    result = land(info, parts[:3], arrived[:3], own[:3], result, "land_three")
    return land(info, parts[3:], arrived[3:], own[3:], result, "land_last")


def solution(mesh):
    return jax.shard_map(
        local, mesh=mesh, in_specs=(P("row", "col"),), out_specs=P("row", "col"), check_vma=False
    )
```

```python
import functools

import jax
import jax.numpy as jnp
from jax import lax
from jax.experimental import pallas as pl
from jax.experimental.pallas import tpu as pltpu
from jax.sharding import PartitionSpec as P

f32, bf16, i32 = jnp.float32, jnp.bfloat16, jnp.int32
AXES = ("row", "col")
VMEM_LIMIT = 16 * 1024 * 1024


def cost(flops, nbytes):
    return pl.CostEstimate(flops=flops // 64, bytes_accessed=nbytes // 64, transcendentals=0)


def split(value):
    high = value.astype(bf16)
    return high, (value - high.astype(f32)).astype(bf16)


def dot(a, b):
    return jnp.dot(a, b, preferred_element_type=f32)


def dot3(a_high, a_low, b_high, b_low):
    return dot(a_high, b_high) + (dot(a_high, b_low) + dot(a_low, b_high))


CORE, SOURCE, SOURCE_PLANE, RING_COL, RING_ROW = range(5)
FAR_FIRST, FAR_SECOND, FAR_HALF, NEAR_HALF, NEAR_FIRST, NEAR_SECOND = range(5, 11)
MOVED_FIRST, MOVED_SECOND, STAYS_FIRST, STAYS_SECOND = range(11, 15)
KEPT_FIRST, KEPT_SECOND, NEAR_BLOCK, FAR_BLOCK = range(15, 19)
LAND_FIRST, LAND_SECOND, END_FIRST, END_SECOND = range(19, 23)
RINGS = (1, 3, 2)


def pack_kernel(info_ref, block_ref, *refs):
    out_refs, packed = refs[:4], refs[4]
    width = block_ref.shape[0]
    half = width // 2
    rows = lax.broadcasted_iota(i32, (half, half), 0)
    cols = lax.broadcasted_iota(i32, (half, half), 1)
    on_diagonal = rows == cols
    top = block_ref[:half, :half]
    bottom = block_ref[half:, half:]
    top_only = jnp.where(on_diagonal, top, 0.0)
    bottom_only = jnp.where(on_diagonal, bottom, 0.0)
    top_down = jnp.sum(top_only, axis=1, keepdims=True)
    top_across = jnp.sum(top_only, axis=0, keepdims=True)
    bottom_down = jnp.sum(bottom_only, axis=1, keepdims=True)
    bottom_across = jnp.sum(bottom_only, axis=0, keepdims=True)
    above = rows < cols
    value = jnp.where(above, top, bottom)
    spacing = jnp.where(above, top_across - top_down, bottom_across - bottom_down)
    packed[:, :half] = jnp.where(
        on_diagonal, 0.0, value / jnp.where(on_diagonal, 1.0, spacing)
    )
    packed[:, half:] = block_ref[:half, half:] / (bottom_across - top_down)
    depth = half // 4
    for out_ref, ring in zip(out_refs, (0,) + RINGS):
        at = pl.multiple_of(lax.rem(info_ref[RING_COL] + ring, 4) * depth, depth)
        out_ref[...] = packed[pl.ds(at, depth), :]


def pack(info, matrix):
    width = matrix.shape[1]
    half = width // 2
    out = jax.ShapeDtypeStruct((half // 4, width), f32)
    out_spec = pl.BlockSpec((half // 4, width), lambda i, info: (0, 0))
    return pl.pallas_call(
        pack_kernel,
        out_shape=[out] * 4,
        grid_spec=pltpu.PrefetchScalarGridSpec(
            num_scalar_prefetch=1,
            grid=(1,),
            in_specs=[pl.BlockSpec((width, width), lambda i, info: (info[CORE], 0))],
            out_specs=[out_spec] * 4,
            scratch_shapes=[pltpu.VMEM((half, width), f32)],
        ),
        compiler_params=pltpu.CompilerParams(vmem_limit_bytes=VMEM_LIMIT),
        cost_estimate=cost(8 * width * width, 6 * width * width),
        name="pack",
    )(info, matrix)


def merge_kernel(info_ref, own, *refs):
    for group in range(2):
        arrived = refs[3 * group : 3 * group + 3]
        total = arrived[0][...] + arrived[1][...] + arrived[2][...]
        refs[6 + group][...] = jnp.where(info_ref[SOURCE] > 0, own[...], total)


def choose_kernel(info_ref, *refs):
    for group in range(2):
        across, held, out = refs[group], refs[2 + group], refs[4 + group]
        out[...] = jnp.where(info_ref[SOURCE_PLANE] > 0, held[...], across[...])


def small(kernel, info, operands, outs, name):
    shape = operands[0].shape
    return pl.pallas_call(
        kernel,
        out_shape=[jax.ShapeDtypeStruct(shape, f32)] * outs,
        in_specs=[pl.BlockSpec(memory_space=pltpu.SMEM)]
        + [pl.BlockSpec(memory_space=pltpu.VMEM)] * len(operands),
        out_specs=[pl.BlockSpec(memory_space=pltpu.VMEM)] * outs,
        compiler_params=pltpu.CompilerParams(vmem_limit_bytes=VMEM_LIMIT),
        cost_estimate=cost(shape[0] * shape[1], 32 * shape[0] * shape[1]),
        name=name,
    )(info, *operands)


def rotation_kernel(sign, in_parts, ring, count, info_ref, *refs):
    outs = refs[-7:-5] if in_parts else refs[-6:-5]
    packed, e_high, e_low, t_high, t_low = refs[-5:]
    half, width = packed.shape
    depth = half // 4
    for k, offset in enumerate((0,) + RINGS):
        at = pl.multiple_of(lax.rem(info_ref[ring] + 4 - offset, 4) * depth, depth)
        if count == 1:
            packed[pl.ds(at, depth), :] = refs[0][k * depth : (k + 1) * depth, :]
        else:
            packed[pl.ds(at, depth), :] = refs[k][...]
    rows = lax.broadcasted_iota(i32, (half, half), 0)
    cols = lax.broadcasted_iota(i32, (half, half), 1)
    triangles = packed[:, :half]
    flipped = -triangles.T
    corner = packed[:, half:]

    def put(r, c, value):
        if sign < 0:
            value = -value
        high, low = split(value)
        e_high[r * half : (r + 1) * half, c * half : (c + 1) * half] = high
        e_low[r * half : (r + 1) * half, c * half : (c + 1) * half] = low

    put(0, 0, jnp.where(rows < cols, triangles, flipped))
    put(1, 1, jnp.where(rows > cols, triangles, flipped))
    put(0, 1, corner)
    put(1, 0, -corner.T)
    tile = 256

    for n in range(width // tile):
        lo, hi = n * tile, (n + 1) * tile
        square = 0.5 * dot3(e_high[:hi, :], e_low[:hi, :], e_high[:, lo:hi], e_low[:, lo:hi])
        t_high[:hi, lo:hi], t_low[:hi, lo:hi] = split(square)
        if n > 0:
            t_high[lo:hi, :lo], t_low[lo:hi, :lo] = split(square[:lo].T)

    def store(r0, r1, c0, c1, value):
        if in_parts:
            outs[0][r0:r1, c0:c1], outs[1][r0:r1, c0:c1] = split(value)
        else:
            outs[0][r0:r1, c0:c1] = value

    for n in range(width // tile):
        lo, hi = n * tile, (n + 1) * tile
        odd = dot3(e_high[:hi, :], e_low[:hi, :], t_high[:, lo:hi], t_low[:, lo:hi])
        odd = odd + (e_high[:hi, lo:hi].astype(f32) + e_low[:hi, lo:hi].astype(f32))
        even = t_high[:hi, lo:hi].astype(f32) + t_low[:hi, lo:hi].astype(f32)
        here = lax.broadcasted_iota(i32, (hi, tile), 0)
        there = lax.broadcasted_iota(i32, (hi, tile), 1) + lo
        store(0, hi, lo, hi, even + odd + jnp.where(here == there, 1.0, 0.0))
        if n > 0:
            store(lo, hi, 0, lo, (even[:lo] - odd[:lo]).T)


def rotation(info, pieces, ring, sign, in_parts, after, name):
    width = pieces[0].shape[1]
    square = (width, width)
    if in_parts:
        shapes = [jax.ShapeDtypeStruct(square, bf16)] * 2
    else:
        shapes = [jax.ShapeDtypeStruct(square, f32)]
    return pl.pallas_call(
        functools.partial(rotation_kernel, sign, in_parts, ring, len(pieces)),
        out_shape=shapes,
        in_specs=[pl.BlockSpec(memory_space=pltpu.SMEM)]
        + [pl.BlockSpec(memory_space=pltpu.VMEM)] * len(pieces)
        + [pl.BlockSpec(memory_space=pl.ANY)] * len(after),
        out_specs=[pl.BlockSpec(memory_space=pltpu.VMEM)] * len(shapes),
        scratch_shapes=[pltpu.VMEM((width // 2, width), f32)] + [pltpu.VMEM(square, bf16)] * 4,
        compiler_params=pltpu.CompilerParams(vmem_limit_bytes=7 * VMEM_LIMIT // 4),
        cost_estimate=cost(12 * width**3, 6 * width * width),
        name=name,
    )(info, *pieces, *after)


def right_kernel(slots, which, info_ref, m_ref, high_ref, low_ref, *refs):
    out_ref = refs[-1]
    width = high_ref.shape[0]
    half = width // 2
    cols = pl.ds(pl.multiple_of(info_ref[which] * half, half), half)
    for k, slot in enumerate(slots):
        rows = pl.ds(pl.multiple_of(info_ref[slot] * width, width), width)
        m_high, m_low = split(m_ref[rows, :])
        out_ref[k * width : (k + 1) * width, :] = dot3(
            m_high, m_low, high_ref[:, cols], low_ref[:, cols]
        )


def right(info, slots, which, matrix, r_high, r_low, after, name):
    width = matrix.shape[1]
    half = width // 2
    return pl.pallas_call(
        functools.partial(right_kernel, slots, which),
        out_shape=jax.ShapeDtypeStruct((len(slots) * width, half), f32),
        in_specs=[pl.BlockSpec(memory_space=pltpu.SMEM)]
        + [pl.BlockSpec(memory_space=pltpu.VMEM)] * 3
        + [pl.BlockSpec(memory_space=pl.ANY)] * len(after),
        out_specs=pl.BlockSpec(memory_space=pltpu.VMEM),
        compiler_params=pltpu.CompilerParams(vmem_limit_bytes=VMEM_LIMIT),
        cost_estimate=cost(3 * len(slots) * width**3, 8 * width * width),
        name=name,
    )(info, matrix, r_high, r_low, *after)


def left_kernel(rows, part_at, info_ref, turned_ref, part_ref, *refs):
    width = turned_ref.shape[0]
    half = width // 2
    at = pl.ds(pl.multiple_of(info_ref[rows] * half, half), half)
    t_high, t_low = split(turned_ref[at, :])
    p_high, p_low = split(part_ref[part_at * width : (part_at + 1) * width, :])
    refs[-1][...] = dot3(t_high, t_low, p_high, p_low)


def left(info, rows, turned, part, part_at, after, name, target=None):
    width = turned.shape[0]
    half = width // 2
    operands = [turned, part] + after
    anywhere = [pl.BlockSpec(memory_space=pl.ANY)] * len(after)
    kernel = functools.partial(left_kernel, rows, part_at)
    limit = VMEM_LIMIT if target is None else 7 * VMEM_LIMIT // 4
    common = dict(
        compiler_params=pltpu.CompilerParams(vmem_limit_bytes=limit),
        cost_estimate=cost(3 * width**3 // 2, 6 * width * width),
        name=name,
    )
    if target is None:
        return pl.pallas_call(
            kernel,
            out_shape=jax.ShapeDtypeStruct((half, half), f32),
            in_specs=[pl.BlockSpec(memory_space=pltpu.SMEM)]
            + [pl.BlockSpec(memory_space=pltpu.VMEM)] * 2
            + anywhere,
            out_specs=pl.BlockSpec(memory_space=pltpu.VMEM),
            **common,
        )(info, *operands)
    row, block, result, shape = target
    aliases = {}
    if result is not None:
        aliases = {1 + len(operands): 0}
        operands.append(result)
        anywhere.append(pl.BlockSpec(memory_space=pl.ANY))
    return pl.pallas_call(
        kernel,
        out_shape=jax.ShapeDtypeStruct(shape, f32),
        grid_spec=pltpu.PrefetchScalarGridSpec(
            num_scalar_prefetch=1,
            grid=(1,),
            in_specs=[
                pl.BlockSpec(turned.shape, lambda i, info: (0, 0)),
                pl.BlockSpec(part.shape, lambda i, info: (0, 0)),
            ]
            + anywhere,
            out_specs=pl.BlockSpec((half, half), lambda i, info: (info[row], info[block])),
        ),
        input_output_aliases=aliases,
        **common,
    )(info, *operands)


def land_kernel(end, info_ref, arrived_ref, own_ref, result_ref, out_ref):
    out_ref[...] = jnp.where(info_ref[end] > 0, own_ref[...], arrived_ref[...])


def land(info, row, block, end, arrived, own, result, name):
    half = arrived.shape[0]
    tile = 256
    per_half = half // tile
    part = pl.BlockSpec((tile, half), lambda i, info: (i, 0))
    return pl.pallas_call(
        functools.partial(land_kernel, end),
        out_shape=jax.ShapeDtypeStruct(result.shape, f32),
        grid_spec=pltpu.PrefetchScalarGridSpec(
            num_scalar_prefetch=1,
            grid=(per_half,),
            in_specs=[part, part, pl.BlockSpec(memory_space=pl.ANY)],
            out_specs=pl.BlockSpec(
                (tile, half), lambda i, info: (info[row] * per_half + i, info[block])
            ),
        ),
        input_output_aliases={3: 0},
        compiler_params=pltpu.CompilerParams(vmem_limit_bytes=VMEM_LIMIT),
        cost_estimate=cost(half * half, 12 * half * half),
        name=name,
    )(info, arrived, own, result)


def group_pairs(group, ring, plane, senders):
    pairs = []
    for row in range(8):
        for col in range(16):
            chip, core = col // 2, col % 2
            if not senders(row, chip):
                continue
            member = row if group == "row" else chip
            member = (member // 4 ^ plane) * 4 + (member + ring) % 4
            target = (member, col) if group == "row" else (row, 2 * member + core)
            pairs.append((row * 16 + col, target[0] * 16 + target[1]))
    return pairs


def is_source(row, chip):
    return row == chip


def in_source_plane(row, chip):
    return row // 4 == chip // 4


def anyone(row, chip):
    return True


def local(matrix):
    row = lax.axis_index("row")
    col = lax.axis_index("col")
    chip = col // 2
    core = col % 2
    rows_here = matrix.shape[0]
    at_end = (col == 0) | (col == 15)
    near_half = jnp.where((core == 1) | (col == 0), 1, 0)
    out_top = jnp.where(row == 0, 0, 1)
    moved_first = jnp.where(core == 0, out_top, 0)
    moved_second = jnp.where(core == 0, 0, out_top)
    values = {
        CORE: core,
        SOURCE: is_source(row, chip),
        SOURCE_PLANE: in_source_plane(row, chip),
        RING_COL: row % 4,
        RING_ROW: chip % 4,
        FAR_FIRST: jnp.where(at_end, core, 1 - core),
        FAR_SECOND: jnp.where(at_end, 1 - core, core),
        FAR_HALF: 1 - near_half,
        NEAR_HALF: near_half,
        NEAR_FIRST: 1 - core,
        NEAR_SECOND: core,
        MOVED_FIRST: moved_first,
        MOVED_SECOND: moved_second,
        STAYS_FIRST: 1 - moved_first,
        STAYS_SECOND: 1 - moved_second,
        KEPT_FIRST: jnp.where(core == 0, 2, 1),
        KEPT_SECOND: jnp.where(core == 0, 1, 2),
        NEAR_BLOCK: 1 - core,
        FAR_BLOCK: core,
        LAND_FIRST: jnp.where(core == 0, 3, 0),
        LAND_SECOND: jnp.where(core == 0, 0, 3),
        END_FIRST: jnp.where(core == 0, row == 7, row == 0),
        END_SECOND: jnp.where(core == 0, row == 0, row == 7),
    }
    info = jnp.stack([jnp.asarray(values[k], i32) for k in range(len(values))])

    own, *quarters = pack(info, matrix)
    arrived = [
        lax.ppermute(quarter, AXES, group_pairs(group, ring, 0, is_source))
        for group in AXES
        for ring, quarter in zip(RINGS, quarters)
    ]
    held = list(small(merge_kernel, info, [own] + arrived, 2, "merge"))
    across = [
        lax.ppermute(one, AXES, group_pairs(group, 0, 1, in_source_plane))
        for group, one in zip(AXES, held)
    ]
    col_own, row_own = small(choose_kernel, info, across + held, 2, "choose")
    col_pieces, row_pieces = (
        [one] + [lax.ppermute(one, AXES, group_pairs(group, ring, 0, anyone)) for ring in RINGS]
        for group, one in zip(AXES, (col_own, row_own))
    )

    swap = [(i, i ^ 1) for i in range(16)]
    row_all = jnp.concatenate(row_pieces, axis=0)
    row_other = lax.ppermute(row_all, "col", swap)

    r_high, r_low = rotation(info, col_pieces, RING_COL, 1, True, [row_all], "column_rotation")
    chips = [(0, 0), (15, 15)]
    chips += [(i, i - 1) for i in range(2, 16, 2)] + [(i, i + 1) for i in range(1, 15, 2)]
    parts = (matrix, r_high, r_low)
    sent = right(info, [FAR_FIRST], FAR_HALF, *parts, [], "right_far_first")
    far_first = lax.ppermute(sent, "col", chips)
    sent = right(info, [NEAR_FIRST, NEAR_SECOND], NEAR_HALF, *parts, [sent], "right_near")
    near = lax.ppermute(sent, "col", swap)
    sent = right(info, [FAR_SECOND], FAR_HALF, *parts, [sent], "right_far_second")
    far_second = lax.ppermute(sent, "col", chips)

    (turned,) = rotation(info, [row_all], RING_ROW, -1, False, [sent], "row_rotation")

    def row_pairs(down_core):
        pairs = []
        for r in range(8):
            for c in range(16):
                target = r - 1 if c % 2 == down_core else r + 1
                if 0 <= target < 8:
                    pairs.append((r * 16 + c, target * 16 + c))
        return pairs

    factors = ((turned, near, 0), (turned, far_first, 0))
    moved, landing, result = [], [], None

    def keep(k, after, result):
        target = (
            (KEPT_FIRST, KEPT_SECOND)[k // 2],
            (NEAR_BLOCK, FAR_BLOCK)[k % 2],
            result,
            (rows_here, matrix.shape[1]),
        )
        rows = (STAYS_FIRST, STAYS_SECOND)[k // 2]
        return left(info, rows, *factors[k], after, "keep_%d" % k, target)

    for k in range(4):
        rows = (MOVED_FIRST, MOVED_SECOND)[k // 2]
        if k == 2:
            (other_turned,) = rotation(
                info, [row_other], RING_ROW, -1, False, moved[1:], "other_row_rotation"
            )
            factors += ((other_turned, near, 1), (other_turned, far_second, 0))
        moved.append(left(info, rows, *factors[k], moved[-1:], "leave_%d" % k))
        landing.append(lax.ppermute(moved[-1], AXES, row_pairs(k // 2)))
    for k in range(4):
        result = keep(k, moved[-1:] if k == 3 else moved[1:2], result)
    for k in range(4):
        result = land(
            info,
            (LAND_FIRST, LAND_SECOND)[k // 2],
            (NEAR_BLOCK, FAR_BLOCK)[k % 2],
            (END_FIRST, END_SECOND)[k // 2],
            landing[k],
            moved[(k + 2) % 4],
            result,
            "land_%d" % k,
        )
    return result


def solution(mesh):
    return jax.shard_map(
        local, mesh=mesh, in_specs=(P("row", "col"),), out_specs=P("row", "col"), check_vma=False
    )
```

```python
import functools

import jax
import jax.numpy as jnp
from jax import lax
from jax.experimental import pallas as pl
from jax.experimental.pallas import tpu as pltpu
from jax.sharding import PartitionSpec as P

f32, bf16, i32 = jnp.float32, jnp.bfloat16, jnp.int32
AXES = ("row", "col")
VMEM_LIMIT = 16 * 1024 * 1024


def cost(flops, nbytes):
    return pl.CostEstimate(flops=flops // 64, bytes_accessed=nbytes // 64, transcendentals=0)


def split(value):
    high = value.astype(bf16)
    return high, (value - high.astype(f32)).astype(bf16)


def dot(a, b):
    return jnp.dot(a, b, preferred_element_type=f32)


def dot3(a_high, a_low, b_high, b_low):
    return dot(a_high, b_high) + (dot(a_high, b_low) + dot(a_low, b_high))


CORE, SOURCE, SOURCE_PLANE, RING_COL, RING_ROW = range(5)
FAR_FIRST, FAR_SECOND, FAR_HALF, NEAR_HALF, NEAR_FIRST, NEAR_SECOND = range(5, 11)
MOVED_FIRST, MOVED_SECOND, STAYS_FIRST, STAYS_SECOND = range(11, 15)
KEPT_FIRST, KEPT_SECOND, NEAR_BLOCK, FAR_BLOCK = range(15, 19)
LAND_FIRST, LAND_SECOND, END_FIRST, END_SECOND = range(19, 23)
RINGS = (1, 3, 2)


def pack_kernel(info_ref, block_ref, *refs):
    out_refs, packed = refs[:4], refs[4]
    width = block_ref.shape[0]
    half = width // 2
    rows = lax.broadcasted_iota(i32, (half, half), 0)
    cols = lax.broadcasted_iota(i32, (half, half), 1)
    on_diagonal = rows == cols
    top = block_ref[:half, :half]
    bottom = block_ref[half:, half:]
    top_only = jnp.where(on_diagonal, top, 0.0)
    bottom_only = jnp.where(on_diagonal, bottom, 0.0)
    top_down = jnp.sum(top_only, axis=1, keepdims=True)
    top_across = jnp.sum(top_only, axis=0, keepdims=True)
    bottom_down = jnp.sum(bottom_only, axis=1, keepdims=True)
    bottom_across = jnp.sum(bottom_only, axis=0, keepdims=True)
    above = rows < cols
    value = jnp.where(above, top, bottom)
    spacing = jnp.where(above, top_across - top_down, bottom_across - bottom_down)
    packed[:, :half] = jnp.where(
        on_diagonal, 0.0, value / jnp.where(on_diagonal, 1.0, spacing)
    )
    packed[:, half:] = block_ref[:half, half:] / (bottom_across - top_down)
    depth = half // 4
    for out_ref, ring in zip(out_refs, (0,) + RINGS):
        at = pl.multiple_of(lax.rem(info_ref[RING_COL] + ring, 4) * depth, depth)
        out_ref[...] = packed[pl.ds(at, depth), :]


def pack(info, matrix):
    width = matrix.shape[1]
    half = width // 2
    out = jax.ShapeDtypeStruct((half // 4, width), f32)
    out_spec = pl.BlockSpec((half // 4, width), lambda i, info: (0, 0))
    return pl.pallas_call(
        pack_kernel,
        out_shape=[out] * 4,
        grid_spec=pltpu.PrefetchScalarGridSpec(
            num_scalar_prefetch=1,
            grid=(1,),
            in_specs=[pl.BlockSpec((width, width), lambda i, info: (info[CORE], 0))],
            out_specs=[out_spec] * 4,
            scratch_shapes=[pltpu.VMEM((half, width), f32)],
        ),
        compiler_params=pltpu.CompilerParams(vmem_limit_bytes=VMEM_LIMIT),
        cost_estimate=cost(8 * width * width, 6 * width * width),
        name="pack",
    )(info, matrix)


def merge_kernel(info_ref, own, *refs):
    for group in range(2):
        arrived = refs[3 * group : 3 * group + 3]
        total = arrived[0][...] + arrived[1][...] + arrived[2][...]
        refs[6 + group][...] = jnp.where(info_ref[SOURCE] > 0, own[...], total)


def choose_kernel(info_ref, across, held, *refs):
    outs = refs[len(refs) // 2 :]
    outs[0][...] = jnp.where(info_ref[SOURCE_PLANE] > 0, held[...], across[...])
    if len(refs) > 1:
        outs[1][...] = refs[0][...]


def small(kernel, info, operands, outs, name):
    shape = operands[0].shape
    return pl.pallas_call(
        kernel,
        out_shape=[jax.ShapeDtypeStruct(shape, f32)] * outs,
        in_specs=[pl.BlockSpec(memory_space=pltpu.SMEM)]
        + [pl.BlockSpec(memory_space=pltpu.VMEM)] * len(operands),
        out_specs=[pl.BlockSpec(memory_space=pltpu.VMEM)] * outs,
        compiler_params=pltpu.CompilerParams(vmem_limit_bytes=VMEM_LIMIT),
        cost_estimate=cost(shape[0] * shape[1], 32 * shape[0] * shape[1]),
        name=name,
    )(info, *operands)


def rotation_kernel(sign, in_parts, ring, count, info_ref, *refs):
    outs = refs[-7:-5] if in_parts else refs[-6:-5]
    packed, e_high, e_low, t_high, t_low = refs[-5:]
    half, width = packed.shape
    depth = half // 4
    for k, offset in enumerate((0,) + RINGS):
        at = pl.multiple_of(lax.rem(info_ref[ring] + 4 - offset, 4) * depth, depth)
        if count == 1:
            packed[pl.ds(at, depth), :] = refs[0][k * depth : (k + 1) * depth, :]
        else:
            packed[pl.ds(at, depth), :] = refs[k][...]
    rows = lax.broadcasted_iota(i32, (half, half), 0)
    cols = lax.broadcasted_iota(i32, (half, half), 1)
    triangles = packed[:, :half]
    flipped = -triangles.T
    corner = packed[:, half:]

    def put(r, c, value):
        if sign < 0:
            value = -value
        high, low = split(value)
        e_high[r * half : (r + 1) * half, c * half : (c + 1) * half] = high
        e_low[r * half : (r + 1) * half, c * half : (c + 1) * half] = low

    put(0, 0, jnp.where(rows < cols, triangles, flipped))
    put(1, 1, jnp.where(rows > cols, triangles, flipped))
    put(0, 1, corner)
    put(1, 0, -corner.T)
    tile = 256

    for n in range(width // tile):
        lo, hi = n * tile, (n + 1) * tile
        square = 0.5 * dot3(e_high[:hi, :], e_low[:hi, :], e_high[:, lo:hi], e_low[:, lo:hi])
        t_high[:hi, lo:hi], t_low[:hi, lo:hi] = split(square)
        if n > 0:
            t_high[lo:hi, :lo], t_low[lo:hi, :lo] = split(square[:lo].T)

    def store(r0, r1, c0, c1, value):
        if in_parts:
            outs[0][r0:r1, c0:c1], outs[1][r0:r1, c0:c1] = split(value)
        else:
            outs[0][r0:r1, c0:c1] = value

    for n in range(width // tile):
        lo, hi = n * tile, (n + 1) * tile
        odd = dot3(e_high[:hi, :], e_low[:hi, :], t_high[:, lo:hi], t_low[:, lo:hi])
        odd = odd + (e_high[:hi, lo:hi].astype(f32) + e_low[:hi, lo:hi].astype(f32))
        even = t_high[:hi, lo:hi].astype(f32) + t_low[:hi, lo:hi].astype(f32)
        here = lax.broadcasted_iota(i32, (hi, tile), 0)
        there = lax.broadcasted_iota(i32, (hi, tile), 1) + lo
        store(0, hi, lo, hi, even + odd + jnp.where(here == there, 1.0, 0.0))
        if n > 0:
            store(lo, hi, 0, lo, (even[:lo] - odd[:lo]).T)


def rotation(info, pieces, ring, sign, in_parts, after, name):
    width = pieces[0].shape[1]
    square = (width, width)
    if in_parts:
        shapes = [jax.ShapeDtypeStruct(square, bf16)] * 2
    else:
        shapes = [jax.ShapeDtypeStruct(square, f32)]
    return pl.pallas_call(
        functools.partial(rotation_kernel, sign, in_parts, ring, len(pieces)),
        out_shape=shapes,
        in_specs=[pl.BlockSpec(memory_space=pltpu.SMEM)]
        + [pl.BlockSpec(memory_space=pltpu.VMEM)] * len(pieces)
        + [pl.BlockSpec(memory_space=pl.ANY)] * len(after),
        out_specs=[pl.BlockSpec(memory_space=pltpu.VMEM)] * len(shapes),
        scratch_shapes=[pltpu.VMEM((width // 2, width), f32)] + [pltpu.VMEM(square, bf16)] * 4,
        compiler_params=pltpu.CompilerParams(vmem_limit_bytes=7 * VMEM_LIMIT // 4),
        cost_estimate=cost(12 * width**3, 6 * width * width),
        name=name,
    )(info, *pieces, *after)


def right_kernel(jobs, info_ref, m_ref, high_ref, low_ref, *refs):
    width = high_ref.shape[0]
    half = width // 2
    for (slots, which), out_ref in zip(jobs, refs[-len(jobs) :]):
        cols = pl.ds(pl.multiple_of(info_ref[which] * half, half), half)
        for k, slot in enumerate(slots):
            rows = pl.ds(pl.multiple_of(info_ref[slot] * width, width), width)
            m_high, m_low = split(m_ref[rows, :])
            out_ref[k * width : (k + 1) * width, :] = dot3(
                m_high, m_low, high_ref[:, cols], low_ref[:, cols]
            )


def right(info, jobs, matrix, r_high, r_low, after, name):
    width = matrix.shape[1]
    half = width // 2
    return pl.pallas_call(
        functools.partial(right_kernel, jobs),
        out_shape=[jax.ShapeDtypeStruct((len(slots) * width, half), f32) for slots, _ in jobs],
        in_specs=[pl.BlockSpec(memory_space=pltpu.SMEM)]
        + [pl.BlockSpec(memory_space=pltpu.VMEM)] * 3
        + [pl.BlockSpec(memory_space=pl.ANY)] * len(after),
        out_specs=[pl.BlockSpec(memory_space=pltpu.VMEM)] * len(jobs),
        compiler_params=pltpu.CompilerParams(vmem_limit_bytes=VMEM_LIMIT),
        cost_estimate=cost(9 * width**3, 8 * width * width),
        name=name,
    )(info, matrix, r_high, r_low, *after)


def left_kernel(rows, part_at, to_result, info_ref, turned_ref, part_ref, *refs):
    width = turned_ref.shape[0]
    half = width // 2
    at = pl.ds(pl.multiple_of(info_ref[rows] * half, half), half)
    t_high, t_low = split(turned_ref[at, :])
    p_high, p_low = split(part_ref[part_at * width : (part_at + 1) * width, :])
    value = dot3(t_high, t_low, p_high, p_low)
    if to_result:
        refs[-2][...] = value
        refs[-1][...] = jnp.zeros_like(refs[-1])
    else:
        refs[-1][...] = value


def left(info, rows, turned, part, part_at, after, name, target=None):
    width = turned.shape[0]
    half = width // 2
    operands = [turned, part] + after
    anywhere = [pl.BlockSpec(memory_space=pl.ANY)] * len(after)
    kernel = functools.partial(left_kernel, rows, part_at, target is not None)
    limit = VMEM_LIMIT if target is None else 7 * VMEM_LIMIT // 4
    common = dict(
        compiler_params=pltpu.CompilerParams(vmem_limit_bytes=limit),
        cost_estimate=cost(3 * width**3 // 2, 6 * width * width),
        name=name,
    )
    if target is None:
        return pl.pallas_call(
            kernel,
            out_shape=jax.ShapeDtypeStruct((half, half), f32),
            in_specs=[pl.BlockSpec(memory_space=pltpu.SMEM)]
            + [pl.BlockSpec(memory_space=pltpu.VMEM)] * 2
            + anywhere,
            out_specs=pl.BlockSpec(memory_space=pltpu.VMEM),
            **common,
        )(info, *operands)
    row, block, result, shape = target
    aliases = {}
    if result is not None:
        aliases = {1 + len(operands): 0}
        operands.append(result)
        anywhere.append(pl.BlockSpec(memory_space=pl.ANY))
    return pl.pallas_call(
        kernel,
        out_shape=[jax.ShapeDtypeStruct(shape, f32), jax.ShapeDtypeStruct((8, 128), f32)],
        grid_spec=pltpu.PrefetchScalarGridSpec(
            num_scalar_prefetch=1,
            grid=(1,),
            in_specs=[
                pl.BlockSpec(turned.shape, lambda i, info: (0, 0)),
                pl.BlockSpec(part.shape, lambda i, info: (0, 0)),
            ]
            + anywhere,
            out_specs=[
                pl.BlockSpec((half, half), lambda i, info: (info[row], info[block])),
                pl.BlockSpec((8, 128), lambda i, info: (0, 0)),
            ],
        ),
        input_output_aliases=aliases,
        **common,
    )(info, *operands)


def land_kernel(end, info_ref, arrived_ref, own_ref, result_ref, out_ref):
    out_ref[...] = jnp.where(info_ref[end] > 0, own_ref[...], arrived_ref[...])


def land(info, row, block, end, arrived, own, result, name):
    half = arrived.shape[0]
    tile = 256
    per_half = half // tile
    part = pl.BlockSpec((tile, half), lambda i, info: (i, 0))
    return pl.pallas_call(
        functools.partial(land_kernel, end),
        out_shape=jax.ShapeDtypeStruct(result.shape, f32),
        grid_spec=pltpu.PrefetchScalarGridSpec(
            num_scalar_prefetch=1,
            grid=(per_half,),
            in_specs=[part, part, pl.BlockSpec(memory_space=pl.ANY)],
            out_specs=pl.BlockSpec(
                (tile, half), lambda i, info: (info[row] * per_half + i, info[block])
            ),
        ),
        input_output_aliases={3: 0},
        compiler_params=pltpu.CompilerParams(vmem_limit_bytes=VMEM_LIMIT),
        cost_estimate=cost(half * half, 12 * half * half),
        name=name,
    )(info, arrived, own, result)


def group_pairs(group, ring, plane, senders):
    pairs = []
    for row in range(8):
        for col in range(16):
            chip, core = col // 2, col % 2
            if not senders(row, chip):
                continue
            member = row if group == "row" else chip
            member = (member // 4 ^ plane) * 4 + (member + ring) % 4
            target = (member, col) if group == "row" else (row, 2 * member + core)
            pairs.append((row * 16 + col, target[0] * 16 + target[1]))
    return pairs


def is_source(row, chip):
    return row == chip


def in_source_plane(row, chip):
    return row // 4 == chip // 4


def anyone(row, chip):
    return True


def local(matrix):
    row = lax.axis_index("row")
    col = lax.axis_index("col")
    chip = col // 2
    core = col % 2
    rows_here = matrix.shape[0]
    at_end = (col == 0) | (col == 15)
    near_half = jnp.where((core == 1) | (col == 0), 1, 0)
    out_top = jnp.where(row == 0, 0, 1)
    moved_first = jnp.where(core == 0, out_top, 0)
    moved_second = jnp.where(core == 0, 0, out_top)
    values = {
        CORE: core,
        SOURCE: is_source(row, chip),
        SOURCE_PLANE: in_source_plane(row, chip),
        RING_COL: row % 4,
        RING_ROW: chip % 4,
        FAR_FIRST: jnp.where(at_end, core, 1 - core),
        FAR_SECOND: jnp.where(at_end, 1 - core, core),
        FAR_HALF: 1 - near_half,
        NEAR_HALF: near_half,
        NEAR_FIRST: 1 - core,
        NEAR_SECOND: core,
        MOVED_FIRST: moved_first,
        MOVED_SECOND: moved_second,
        STAYS_FIRST: 1 - moved_first,
        STAYS_SECOND: 1 - moved_second,
        KEPT_FIRST: jnp.where(core == 0, 2, 1),
        KEPT_SECOND: jnp.where(core == 0, 1, 2),
        NEAR_BLOCK: 1 - core,
        FAR_BLOCK: core,
        LAND_FIRST: jnp.where(core == 0, 3, 0),
        LAND_SECOND: jnp.where(core == 0, 0, 3),
        END_FIRST: jnp.where(core == 0, row == 7, row == 0),
        END_SECOND: jnp.where(core == 0, row == 0, row == 7),
    }
    info = jnp.stack([jnp.asarray(values[k], i32) for k in range(len(values))])

    own, *quarters = pack(info, matrix)
    arrived = [
        lax.ppermute(quarter, AXES, group_pairs(group, ring, 0, is_source))
        for group in AXES
        for ring, quarter in zip(RINGS, quarters)
    ]
    held = list(small(merge_kernel, info, [own] + arrived, 2, "merge"))
    def cross(group, one):
        return lax.ppermute(one, AXES, group_pairs(group, 0, 1, in_source_plane))

    def around(group, one):
        return [one] + [
            lax.ppermute(one, AXES, group_pairs(group, ring, 0, anyone)) for ring in RINGS
        ]

    col_held, row_held = held
    col_own, row_held = small(
        choose_kernel, info, [cross("row", col_held), col_held, row_held], 2, "choose_col"
    )
    col_pieces = around("row", col_own)
    (row_own,) = small(choose_kernel, info, [cross("col", row_held), row_held], 1, "choose_row")
    row_pieces = around("col", row_own)

    swap = [(i, i ^ 1) for i in range(16)]
    chips = [(0, 0), (15, 15)]
    chips += [(i, i - 1) for i in range(2, 16, 2)] + [(i, i + 1) for i in range(1, 15, 2)]

    def row_pairs(down_core):
        pairs = []
        for r in range(8):
            for c in range(16):
                target = r - 1 if c % 2 == down_core else r + 1
                if 0 <= target < 8:
                    pairs.append((r * 16 + c, target * 16 + c))
        return pairs

    def leave(k, turned, part, part_at, after):
        rows = (MOVED_FIRST, MOVED_SECOND)[k // 2]
        moved = left(info, rows, turned, part, part_at, after, "leave_%d" % k)
        return moved, lax.ppermute(moved, AXES, row_pairs(k // 2))

    def keep(k, turned, part, part_at, after, result):
        target = (
            (KEPT_FIRST, KEPT_SECOND)[k // 2],
            (NEAR_BLOCK, FAR_BLOCK)[k % 2],
            result,
            (rows_here, matrix.shape[1]),
        )
        rows = (STAYS_FIRST, STAYS_SECOND)[k // 2]
        return left(info, rows, turned, part, part_at, after, "keep_%d" % k, target)

    row_all = jnp.concatenate(row_pieces, axis=0)
    row_other = lax.ppermute(row_all, "col", swap)
    r_high, r_low = rotation(info, col_pieces, RING_COL, 1, True, [row_own], "column_rotation")
    factors = (matrix, r_high, r_low)
    parts = []
    for slot, which, name in (
        (FAR_FIRST, FAR_HALF, "right_far_first"),
        (FAR_SECOND, FAR_HALF, "right_far_second"),
        (NEAR_FIRST, NEAR_HALF, "right_near_first"),
        (NEAR_SECOND, NEAR_HALF, "right_near_second"),
    ):
        after = parts[-1:] if parts else [row_all]
        (sent,) = right(info, [([slot], which)], *factors, after, name)
        parts.append(sent)
    far_first, far_second = (lax.ppermute(part, "col", chips) for part in parts[:2])
    near_first, near_second = (lax.ppermute(part, "col", swap) for part in parts[2:])
    (turned,) = rotation(info, [row_all], RING_ROW, -1, False, parts[3:], "row_rotation")
    moved, landing = [None] * 4, [None] * 4
    moved[1], landing[1] = leave(1, turned, far_first, 0, [])
    moved[0], landing[0] = leave(0, turned, near_first, 0, [moved[1]])
    (other_turned,) = rotation(
        info, [row_other], RING_ROW, -1, False, [moved[0]], "other_row_rotation"
    )
    moved[2], landing[2] = leave(2, other_turned, near_second, 0, [])
    result, _ = keep(0, turned, near_first, 0, [moved[2]], None)
    result, _ = keep(1, turned, far_first, 0, [], result)
    result, token = keep(2, other_turned, near_second, 0, [], result)
    moved[3], landing[3] = leave(3, other_turned, far_second, 0, [token])
    result, _ = keep(3, other_turned, far_second, 0, [moved[3]], result)
    for k in range(4):
        result = land(
            info,
            (LAND_FIRST, LAND_SECOND)[k // 2],
            (NEAR_BLOCK, FAR_BLOCK)[k % 2],
            (END_FIRST, END_SECOND)[k // 2],
            landing[k],
            moved[(k + 2) % 4],
            result,
            "land_%d" % k,
        )
    return result


def solution(mesh):
    return jax.shard_map(
        local, mesh=mesh, in_specs=(P("row", "col"),), out_specs=P("row", "col"), check_vma=False
    )
```

```python
import functools

import jax
import jax.numpy as jnp
from jax import lax
from jax.experimental import pallas as pl
from jax.experimental.pallas import tpu as pltpu
from jax.sharding import PartitionSpec as P

f32, bf16, i32 = jnp.float32, jnp.bfloat16, jnp.int32
AXES = ("row", "col")
VMEM_LIMIT = 16 * 1024 * 1024


def cost(flops, nbytes, share=1 / 64):
    return pl.CostEstimate(
        flops=int(flops * share), bytes_accessed=int(nbytes * share), transcendentals=0
    )


LEFT_SHARE = 16


def split(value):
    high = value.astype(bf16)
    return high, (value - high.astype(f32)).astype(bf16)


def dot(a, b):
    return jnp.dot(a, b, preferred_element_type=f32)


def dot3(a_high, a_low, b_high, b_low):
    return dot(a_high, b_high) + (dot(a_high, b_low) + dot(a_low, b_high))


CORE, SOURCE, SOURCE_PLANE, RING_COL, RING_ROW = range(5)
FAR_FIRST, FAR_SECOND, FAR_HALF, NEAR_HALF, NEAR_FIRST, NEAR_SECOND = range(5, 11)
MOVED_FIRST, MOVED_SECOND, STAYS_FIRST, STAYS_SECOND = range(11, 15)
KEPT_FIRST, KEPT_SECOND, NEAR_BLOCK, FAR_BLOCK = range(15, 19)
LAND_FIRST, LAND_SECOND, END_FIRST, END_SECOND, END_COL = range(19, 24)
RINGS = (1, 3, 2)


def pack_kernel(info_ref, block_ref, *refs):
    out_refs, packed = refs[:4], refs[4]
    width = block_ref.shape[0]
    half = width // 2
    rows = lax.broadcasted_iota(i32, (half, half), 0)
    cols = lax.broadcasted_iota(i32, (half, half), 1)
    on_diagonal = rows == cols
    top = block_ref[:half, :half]
    bottom = block_ref[half:, half:]
    top_only = jnp.where(on_diagonal, top, 0.0)
    bottom_only = jnp.where(on_diagonal, bottom, 0.0)
    top_down = jnp.sum(top_only, axis=1, keepdims=True)
    top_across = jnp.sum(top_only, axis=0, keepdims=True)
    bottom_down = jnp.sum(bottom_only, axis=1, keepdims=True)
    bottom_across = jnp.sum(bottom_only, axis=0, keepdims=True)
    above = rows < cols
    value = jnp.where(above, top, bottom)
    spacing = jnp.where(above, top_across - top_down, bottom_across - bottom_down)
    packed[:, :half] = jnp.where(
        on_diagonal, 0.0, value / jnp.where(on_diagonal, 1.0, spacing)
    )
    packed[:, half:] = block_ref[:half, half:] / (bottom_across - top_down)
    depth = half // 4
    for out_ref, ring in zip(out_refs, (0,) + RINGS):
        at = pl.multiple_of(lax.rem(info_ref[RING_COL] + ring, 4) * depth, depth)
        out_ref[...] = packed[pl.ds(at, depth), :]


def pack(info, matrix):
    width = matrix.shape[1]
    half = width // 2
    out = jax.ShapeDtypeStruct((half // 4, width), f32)
    out_spec = pl.BlockSpec((half // 4, width), lambda i, info: (0, 0))
    return pl.pallas_call(
        pack_kernel,
        out_shape=[out] * 4,
        grid_spec=pltpu.PrefetchScalarGridSpec(
            num_scalar_prefetch=1,
            grid=(1,),
            in_specs=[pl.BlockSpec((width, width), lambda i, info: (info[CORE], 0))],
            out_specs=[out_spec] * 4,
            scratch_shapes=[pltpu.VMEM((half, width), f32)],
        ),
        compiler_params=pltpu.CompilerParams(vmem_limit_bytes=VMEM_LIMIT),
        cost_estimate=cost(8 * width * width, 6 * width * width),
        name="pack",
    )(info, matrix)


def merge_kernel(info_ref, own, *refs):
    for group in range(2):
        arrived = refs[3 * group : 3 * group + 3]
        total = arrived[0][...] + arrived[1][...] + arrived[2][...]
        refs[6 + group][...] = jnp.where(info_ref[SOURCE] > 0, own[...], total)


def choose_kernel(info_ref, across, held, *refs):
    outs = refs[len(refs) // 2 :]
    outs[0][...] = jnp.where(info_ref[SOURCE_PLANE] > 0, held[...], across[...])
    if len(refs) > 1:
        outs[1][...] = refs[0][...]


def stack_kernel(info_ref, top, bottom, after, out):
    rows = top.shape[0]
    out[:rows, :] = top[...]
    out[rows:, :] = bottom[...]


def stacked(info, top, bottom, after):
    rows, width = top.shape
    return pl.pallas_call(
        stack_kernel,
        out_shape=jax.ShapeDtypeStruct((2 * rows, width), f32),
        in_specs=[pl.BlockSpec(memory_space=pltpu.SMEM)]
        + [pl.BlockSpec(memory_space=pltpu.VMEM)] * 2
        + [pl.BlockSpec(memory_space=pl.ANY)],
        out_specs=pl.BlockSpec(memory_space=pltpu.VMEM),
        compiler_params=pltpu.CompilerParams(vmem_limit_bytes=VMEM_LIMIT),
        cost_estimate=cost(rows * width, 16 * rows * width),
        name="stacked",
    )(info, top, bottom, after)


def small(kernel, info, operands, outs, name):
    shape = operands[0].shape
    return pl.pallas_call(
        kernel,
        out_shape=[jax.ShapeDtypeStruct(shape, f32)] * outs,
        in_specs=[pl.BlockSpec(memory_space=pltpu.SMEM)]
        + [pl.BlockSpec(memory_space=pltpu.VMEM)] * len(operands),
        out_specs=[pl.BlockSpec(memory_space=pltpu.VMEM)] * outs,
        compiler_params=pltpu.CompilerParams(vmem_limit_bytes=VMEM_LIMIT),
        cost_estimate=cost(shape[0] * shape[1], 32 * shape[0] * shape[1]),
        name=name,
    )(info, *operands)


def rotation_kernel(sign, in_parts, ring, count, info_ref, *refs):
    outs = refs[-7:-5] if in_parts else refs[-6:-5]
    packed, e_high, e_low, t_high, t_low = refs[-5:]
    half, width = packed.shape
    depth = half // 4
    for k, offset in enumerate((0,) + RINGS):
        at = pl.multiple_of(lax.rem(info_ref[ring] + 4 - offset, 4) * depth, depth)
        if count == 1:
            packed[pl.ds(at, depth), :] = refs[0][k * depth : (k + 1) * depth, :]
        else:
            packed[pl.ds(at, depth), :] = refs[k][...]
    rows = lax.broadcasted_iota(i32, (half, half), 0)
    cols = lax.broadcasted_iota(i32, (half, half), 1)
    triangles = packed[:, :half]
    flipped = -triangles.T
    corner = packed[:, half:]

    def put(r, c, value):
        if sign < 0:
            value = -value
        high, low = split(value)
        e_high[r * half : (r + 1) * half, c * half : (c + 1) * half] = high
        e_low[r * half : (r + 1) * half, c * half : (c + 1) * half] = low

    put(0, 0, jnp.where(rows < cols, triangles, flipped))
    put(1, 1, jnp.where(rows > cols, triangles, flipped))
    put(0, 1, corner)
    put(1, 0, -corner.T)
    tile = 256

    for n in range(width // tile):
        lo, hi = n * tile, (n + 1) * tile
        square = 0.5 * dot3(e_high[:hi, :], e_low[:hi, :], e_high[:, lo:hi], e_low[:, lo:hi])
        t_high[:hi, lo:hi], t_low[:hi, lo:hi] = split(square)
        if n > 0:
            t_high[lo:hi, :lo], t_low[lo:hi, :lo] = split(square[:lo].T)

    def store(r0, r1, c0, c1, value):
        if in_parts:
            outs[0][r0:r1, c0:c1], outs[1][r0:r1, c0:c1] = split(value)
        else:
            outs[0][r0:r1, c0:c1] = value

    for n in range(width // tile):
        lo, hi = n * tile, (n + 1) * tile
        odd = dot3(e_high[:hi, :], e_low[:hi, :], t_high[:, lo:hi], t_low[:, lo:hi])
        odd = odd + (e_high[:hi, lo:hi].astype(f32) + e_low[:hi, lo:hi].astype(f32))
        even = t_high[:hi, lo:hi].astype(f32) + t_low[:hi, lo:hi].astype(f32)
        here = lax.broadcasted_iota(i32, (hi, tile), 0)
        there = lax.broadcasted_iota(i32, (hi, tile), 1) + lo
        store(0, hi, lo, hi, even + odd + jnp.where(here == there, 1.0, 0.0))
        if n > 0:
            store(lo, hi, 0, lo, (even[:lo] - odd[:lo]).T)


def rotation(info, pieces, ring, sign, in_parts, after, name):
    width = pieces[0].shape[1]
    square = (width, width)
    if in_parts:
        shapes = [jax.ShapeDtypeStruct(square, bf16)] * 2
    else:
        shapes = [jax.ShapeDtypeStruct(square, f32)]
    return pl.pallas_call(
        functools.partial(rotation_kernel, sign, in_parts, ring, len(pieces)),
        out_shape=shapes,
        in_specs=[pl.BlockSpec(memory_space=pltpu.SMEM)]
        + [pl.BlockSpec(memory_space=pltpu.VMEM)] * len(pieces)
        + [pl.BlockSpec(memory_space=pl.ANY)] * len(after),
        out_specs=[pl.BlockSpec(memory_space=pltpu.VMEM)] * len(shapes),
        scratch_shapes=[pltpu.VMEM((width // 2, width), f32)] + [pltpu.VMEM(square, bf16)] * 4,
        compiler_params=pltpu.CompilerParams(vmem_limit_bytes=5 * VMEM_LIMIT // 4),
        cost_estimate=cost(12 * width**3, 6 * width * width),
        name=name,
    )(info, *pieces, *after)


def right_kernel(jobs, info_ref, m_ref, high_ref, low_ref, *refs):
    width = high_ref.shape[0]
    half = width // 2
    for (slots, which), out_ref in zip(jobs, refs[-len(jobs) :]):
        cols = pl.ds(pl.multiple_of(info_ref[which] * half, half), half)
        for k, slot in enumerate(slots):
            rows = pl.ds(pl.multiple_of(info_ref[slot] * width, width), width)
            m_high, m_low = split(m_ref[rows, :])
            out_ref[k * width : (k + 1) * width, :] = dot3(
                m_high, m_low, high_ref[:, cols], low_ref[:, cols]
            )


def right(info, jobs, matrix, r_high, r_low, after, name):
    width = matrix.shape[1]
    half = width // 2
    return pl.pallas_call(
        functools.partial(right_kernel, jobs),
        out_shape=[jax.ShapeDtypeStruct((len(slots) * width, half), f32) for slots, _ in jobs],
        in_specs=[pl.BlockSpec(memory_space=pltpu.SMEM)]
        + [pl.BlockSpec(memory_space=pltpu.VMEM)] * 3
        + [pl.BlockSpec(memory_space=pl.ANY)] * len(after),
        out_specs=[pl.BlockSpec(memory_space=pltpu.VMEM)] * len(jobs),
        compiler_params=pltpu.CompilerParams(vmem_limit_bytes=VMEM_LIMIT),
        cost_estimate=cost(9 * width**3, 8 * width * width),
        name=name,
    )(info, matrix, r_high, r_low, *after)


def left_kernel(rows, place, info_ref, turned_ref, part_ref, own_ref, *refs):
    width = turned_ref.shape[0]
    half = width // 2
    at = pl.ds(pl.multiple_of(info_ref[rows] * half, half), half)
    t_high, t_low = split(turned_ref[at, :])
    part = part_ref[...]
    if own_ref is not part_ref:
        part = jnp.where(info_ref[END_COL] > 0, own_ref[...], part)
    value = dot3(t_high, t_low, *split(part))
    if place is None:
        refs[-1][...] = value
        return
    out_ref, token_ref, kept, sem = refs[-4:]
    kept[...] = value
    row, block = place
    out_rows = pl.ds(pl.multiple_of(info_ref[row] * half, half), half)
    out_cols = pl.ds(pl.multiple_of(info_ref[block] * half, half), half)
    copy = pltpu.make_async_copy(kept, out_ref.at[out_rows, out_cols], sem)
    copy.start()
    token_ref[...] = jnp.zeros_like(token_ref)
    copy.wait()


def near_kernel(rows, place, info_ref, turned_ref, part_ref, *refs):
    left_kernel(rows, place, info_ref, turned_ref, part_ref, part_ref, *refs)


def left(info, rows, turned, part, after, name, target=None):
    width = turned.shape[0]
    half = width // 2
    operands = [turned] + list(part) + after
    in_specs = [pl.BlockSpec(memory_space=pltpu.SMEM)]
    in_specs += [pl.BlockSpec(memory_space=pltpu.VMEM)] * (1 + len(part))
    in_specs += [pl.BlockSpec(memory_space=pl.ANY)] * len(after)
    kernel = left_kernel if len(part) > 1 else near_kernel
    common = dict(
        compiler_params=pltpu.CompilerParams(vmem_limit_bytes=VMEM_LIMIT),
        cost_estimate=cost(3 * width**3 // 2, 6 * width * width, LEFT_SHARE),
        name=name,
    )
    if target is None:
        return pl.pallas_call(
            functools.partial(kernel, rows, None),
            out_shape=jax.ShapeDtypeStruct((half, half), f32),
            in_specs=in_specs,
            out_specs=pl.BlockSpec(memory_space=pltpu.VMEM),
            **common,
        )(info, *operands)
    row, block, result, shape = target
    aliases = {}
    if result is not None:
        aliases = {1 + len(operands): 0}
        operands.append(result)
        in_specs.append(pl.BlockSpec(memory_space=pl.ANY))
    return pl.pallas_call(
        functools.partial(kernel, rows, (row, block)),
        out_shape=[jax.ShapeDtypeStruct(shape, f32), jax.ShapeDtypeStruct((8, 128), f32)],
        in_specs=in_specs,
        out_specs=[pl.BlockSpec(memory_space=pl.ANY), pl.BlockSpec(memory_space=pltpu.VMEM)],
        scratch_shapes=[pltpu.VMEM((half, half), f32), pltpu.SemaphoreType.DMA],
        input_output_aliases=aliases,
        **common,
    )(info, *operands)


def land_kernel(end, info_ref, arrived_ref, own_ref, *refs):
    arrived = arrived_ref[...]
    if len(refs) > 2:
        arrived = arrived + refs[0][...]
    refs[-1][...] = jnp.where(info_ref[end] > 0, own_ref[...], arrived)


def land(info, row, block, end, arrived, own, late, result, name):
    half = arrived.shape[0]
    tile = 256
    per_half = half // tile
    part = pl.BlockSpec((tile, half), lambda i, info: (i, 0))
    operands, in_specs = [arrived, own], [part, part]
    if late is not None:
        late, late_at = late
        operands.append(late)
        in_specs.append(pl.BlockSpec((tile, half), lambda i, info: (late_at * per_half + i, 0)))
    return pl.pallas_call(
        functools.partial(land_kernel, end),
        out_shape=jax.ShapeDtypeStruct(result.shape, f32),
        grid_spec=pltpu.PrefetchScalarGridSpec(
            num_scalar_prefetch=1,
            grid=(per_half,),
            in_specs=in_specs + [pl.BlockSpec(memory_space=pl.ANY)],
            out_specs=pl.BlockSpec(
                (tile, half), lambda i, info: (info[row] * per_half + i, info[block])
            ),
        ),
        input_output_aliases={1 + len(operands): 0},
        compiler_params=pltpu.CompilerParams(vmem_limit_bytes=VMEM_LIMIT),
        cost_estimate=cost(half * half, 12 * half * half),
        name=name,
    )(info, *operands, result)


def group_pairs(group, ring, plane, senders):
    pairs = []
    for row in range(8):
        for col in range(16):
            chip, core = col // 2, col % 2
            if not senders(row, chip):
                continue
            member = row if group == "row" else chip
            member = (member // 4 ^ plane) * 4 + (member + ring) % 4
            target = (member, col) if group == "row" else (row, 2 * member + core)
            pairs.append((row * 16 + col, target[0] * 16 + target[1]))
    return pairs


def is_source(row, chip):
    return row == chip


def in_source_plane(row, chip):
    return row // 4 == chip // 4


def anyone(row, chip):
    return True


def local(matrix):
    row = lax.axis_index("row")
    col = lax.axis_index("col")
    chip = col // 2
    core = col % 2
    rows_here = matrix.shape[0]
    at_end = (col == 0) | (col == 15)
    near_half = jnp.where((core == 1) | (col == 0), 1, 0)
    out_top = jnp.where(row == 0, 0, 1)
    moved_first = jnp.where(core == 0, out_top, 0)
    moved_second = jnp.where(core == 0, 0, out_top)
    values = {
        CORE: core,
        SOURCE: is_source(row, chip),
        SOURCE_PLANE: in_source_plane(row, chip),
        RING_COL: row % 4,
        RING_ROW: chip % 4,
        FAR_FIRST: jnp.where(at_end, core, 1 - core),
        FAR_SECOND: jnp.where(at_end, 1 - core, core),
        FAR_HALF: 1 - near_half,
        NEAR_HALF: near_half,
        NEAR_FIRST: 1 - core,
        NEAR_SECOND: core,
        MOVED_FIRST: moved_first,
        MOVED_SECOND: moved_second,
        STAYS_FIRST: 1 - moved_first,
        STAYS_SECOND: 1 - moved_second,
        KEPT_FIRST: jnp.where(core == 0, 2, 1),
        KEPT_SECOND: jnp.where(core == 0, 1, 2),
        NEAR_BLOCK: 1 - core,
        FAR_BLOCK: core,
        LAND_FIRST: jnp.where(core == 0, 3, 0),
        LAND_SECOND: jnp.where(core == 0, 0, 3),
        END_FIRST: jnp.where(core == 0, row == 7, row == 0),
        END_SECOND: jnp.where(core == 0, row == 0, row == 7),
        END_COL: at_end,
    }
    info = jnp.stack([jnp.asarray(values[k], i32) for k in range(len(values))])

    own, *quarters = pack(info, matrix)
    arrived = [
        lax.ppermute(quarter, AXES, group_pairs(group, ring, 0, is_source))
        for group in AXES
        for ring, quarter in zip(RINGS, quarters)
    ]
    held = list(small(merge_kernel, info, [own] + arrived, 2, "merge"))
    def cross(group, one):
        return lax.ppermute(one, AXES, group_pairs(group, 0, 1, in_source_plane))

    def around(group, one):
        return [one] + [
            lax.ppermute(one, AXES, group_pairs(group, ring, 0, anyone)) for ring in RINGS
        ]

    col_held, row_held = held
    col_own, row_held = small(
        choose_kernel, info, [cross("row", col_held), col_held, row_held], 2, "choose_col"
    )
    col_pieces = around("row", col_own)
    (row_own,) = small(choose_kernel, info, [cross("col", row_held), row_held], 1, "choose_row")
    row_pieces = around("col", row_own)

    swap = [(i, i ^ 1) for i in range(16)]
    chips = [(i, i - 1) for i in range(2, 16, 2)] + [(i, i + 1) for i in range(1, 15, 2)]

    def row_pairs(down_core, middle, others):
        pairs = []
        for r in range(8):
            for c in range(16):
                target = r - 1 if c % 2 == down_core else r + 1
                if 0 <= target < 8 and (middle if {r, target} == {3, 4} else others):
                    pairs.append((r * 16 + c, target * 16 + c))
        return pairs

    def leave(k, turned, part, after):
        rows = (MOVED_FIRST, MOVED_SECOND)[k // 2]
        moved = left(info, rows, turned, part, after, "leave_%d" % k)
        return moved, lax.ppermute(moved, AXES, row_pairs(k // 2, k // 2 == 1, True))

    def keep(k, turned, part, after, result):
        target = (
            (KEPT_FIRST, KEPT_SECOND)[k // 2],
            (NEAR_BLOCK, FAR_BLOCK)[k % 2],
            result,
            (rows_here, matrix.shape[1]),
        )
        rows = (STAYS_FIRST, STAYS_SECOND)[k // 2]
        return left(info, rows, turned, part, after, "keep_%d" % k, target)

    row_all = jnp.concatenate(row_pieces, axis=0)
    row_other = lax.ppermute(row_all, "col", swap)
    r_high, r_low = rotation(info, col_pieces, RING_COL, 1, True, [row_own], "column_rotation")
    factors = (matrix, r_high, r_low)
    parts = []
    for slot, which, name in (
        (FAR_FIRST, FAR_HALF, "right_far_first"),
        (FAR_SECOND, FAR_HALF, "right_far_second"),
        (NEAR_FIRST, NEAR_HALF, "right_near_first"),
        (NEAR_SECOND, NEAR_HALF, "right_near_second"),
    ):
        after = parts[-1:] if parts else [row_all]
        (sent,) = right(info, [([slot], which)], *factors, after, name)
        parts.append(sent)
    far_first, far_second = ((lax.ppermute(part, "col", chips), part) for part in parts[:2])
    near_first, near_second = ((lax.ppermute(part, "col", swap),) for part in parts[2:])
    (turned,) = rotation(info, [row_all], RING_ROW, -1, False, parts[3:], "row_rotation")
    moved, landing = [None] * 4, [None] * 4
    moved[1], landing[1] = leave(1, turned, far_first, [])
    moved[0], landing[0] = leave(0, turned, near_first, [moved[1]])
    late = stacked(info, moved[0], moved[1], moved[0])
    (other_turned,) = rotation(
        info, [row_other], RING_ROW, -1, False, [late], "other_row_rotation"
    )
    late = lax.ppermute(late, AXES, row_pairs(0, True, False))
    moved[2], landing[2] = leave(2, other_turned, near_second, [])
    result, token = keep(0, turned, near_first, [moved[2]], None)
    moved[3], landing[3] = leave(3, other_turned, far_second, [token])
    result, _ = keep(1, turned, far_first, [moved[3], landing[1]], result)
    result, _ = keep(2, other_turned, near_second, [landing[0]], result)
    result, _ = keep(3, other_turned, far_second, [], result)
    for k in (2, 0, 1, 3):
        result = land(
            info,
            (LAND_FIRST, LAND_SECOND)[k // 2],
            (NEAR_BLOCK, FAR_BLOCK)[k % 2],
            (END_FIRST, END_SECOND)[k // 2],
            landing[k],
            moved[(k + 2) % 4],
            (late, k) if k < 2 else None,
            result,
            "land_%d" % k,
        )
    return result


def solution(mesh):
    return jax.shard_map(
        local, mesh=mesh, in_specs=(P("row", "col"),), out_specs=P("row", "col"), check_vma=False
    )
```

```python
import functools

import jax
import jax.numpy as jnp
from jax import lax
from jax.experimental import pallas as pl
from jax.experimental.pallas import tpu as pltpu
from jax.sharding import PartitionSpec as P

f32, bf16, i32 = jnp.float32, jnp.bfloat16, jnp.int32
AXES = ("row", "col")
VMEM_LIMIT = 16 * 1024 * 1024


def cost(flops, nbytes, share=1 / 64):
    return pl.CostEstimate(
        flops=int(flops * share), bytes_accessed=int(nbytes * share), transcendentals=0
    )


LEFT_SHARE = 16


def split(value):
    high = value.astype(bf16)
    return high, (value - high.astype(f32)).astype(bf16)


def dot(a, b):
    return jnp.dot(a, b, preferred_element_type=f32)


def dot3(a_high, a_low, b_high, b_low):
    return dot(a_high, b_high) + (dot(a_high, b_low) + dot(a_low, b_high))


CORE, SOURCE, SOURCE_PLANE, RING_COL, RING_ROW = range(5)
FAR_FIRST, FAR_SECOND, FAR_HALF, NEAR_HALF, NEAR_FIRST, NEAR_SECOND = range(5, 11)
MOVED_FIRST, MOVED_SECOND, STAYS_FIRST, STAYS_SECOND = range(11, 15)
KEPT_FIRST, KEPT_SECOND, NEAR_BLOCK, FAR_BLOCK = range(15, 19)
LAND_FIRST, LAND_SECOND, END_FIRST, END_SECOND, END_COL = range(19, 24)
HAS_LATE, HAS_HOP = range(24, 26)
RINGS = (1, 3, 2)


def pack_kernel(info_ref, block_ref, *refs):
    out_refs, packed = refs[:4], refs[4]
    width = block_ref.shape[0]
    half = width // 2
    rows = lax.broadcasted_iota(i32, (half, half), 0)
    cols = lax.broadcasted_iota(i32, (half, half), 1)
    on_diagonal = rows == cols
    top = block_ref[:half, :half]
    bottom = block_ref[half:, half:]
    top_only = jnp.where(on_diagonal, top, 0.0)
    bottom_only = jnp.where(on_diagonal, bottom, 0.0)
    top_down = jnp.sum(top_only, axis=1, keepdims=True)
    top_across = jnp.sum(top_only, axis=0, keepdims=True)
    bottom_down = jnp.sum(bottom_only, axis=1, keepdims=True)
    bottom_across = jnp.sum(bottom_only, axis=0, keepdims=True)
    above = rows < cols
    value = jnp.where(above, top, bottom)
    spacing = jnp.where(above, top_across - top_down, bottom_across - bottom_down)
    packed[:, :half] = jnp.where(
        on_diagonal, 0.0, value / jnp.where(on_diagonal, 1.0, spacing)
    )
    packed[:, half:] = block_ref[:half, half:] / (bottom_across - top_down)
    depth = half // 4
    for out_ref, ring in zip(out_refs, (0,) + RINGS):
        at = pl.multiple_of(lax.rem(info_ref[RING_COL] + ring, 4) * depth, depth)
        out_ref[...] = packed[pl.ds(at, depth), :]


def pack(info, matrix):
    width = matrix.shape[1]
    half = width // 2
    out = jax.ShapeDtypeStruct((half // 4, width), f32)
    out_spec = pl.BlockSpec((half // 4, width), lambda i, info: (0, 0))
    return pl.pallas_call(
        pack_kernel,
        out_shape=[out] * 4,
        grid_spec=pltpu.PrefetchScalarGridSpec(
            num_scalar_prefetch=1,
            grid=(1,),
            in_specs=[pl.BlockSpec((width, width), lambda i, info: (info[CORE], 0))],
            out_specs=[out_spec] * 4,
            scratch_shapes=[pltpu.VMEM((half, width), f32)],
        ),
        compiler_params=pltpu.CompilerParams(vmem_limit_bytes=VMEM_LIMIT),
        cost_estimate=cost(8 * width * width, 6 * width * width),
        name="pack",
    )(info, matrix)


def merge_kernel(info_ref, own, *refs):
    for group in range(2):
        arrived = refs[3 * group : 3 * group + 3]
        total = arrived[0][...] + arrived[1][...] + arrived[2][...]
        refs[6 + group][...] = jnp.where(info_ref[SOURCE] > 0, own[...], total)


def choose_kernel(info_ref, across, held, *refs):
    outs = refs[len(refs) // 2 :]
    outs[0][...] = jnp.where(info_ref[SOURCE_PLANE] > 0, held[...], across[...])
    if len(refs) > 1:
        outs[1][...] = refs[0][...]


def stack_kernel(info_ref, top, bottom, after, out):
    rows = top.shape[0]
    out[:rows, :] = top[...]
    out[rows:, :] = bottom[...]


def stacked(info, top, bottom, after):
    rows, width = top.shape
    return pl.pallas_call(
        stack_kernel,
        out_shape=jax.ShapeDtypeStruct((2 * rows, width), f32),
        in_specs=[pl.BlockSpec(memory_space=pltpu.SMEM)]
        + [pl.BlockSpec(memory_space=pltpu.VMEM)] * 2
        + [pl.BlockSpec(memory_space=pl.ANY)],
        out_specs=pl.BlockSpec(memory_space=pltpu.VMEM),
        compiler_params=pltpu.CompilerParams(vmem_limit_bytes=VMEM_LIMIT),
        cost_estimate=cost(rows * width, 16 * rows * width),
        name="stacked",
    )(info, top, bottom, after)


def small(kernel, info, operands, outs, name):
    shape = operands[0].shape
    return pl.pallas_call(
        kernel,
        out_shape=[jax.ShapeDtypeStruct(shape, f32)] * outs,
        in_specs=[pl.BlockSpec(memory_space=pltpu.SMEM)]
        + [pl.BlockSpec(memory_space=pltpu.VMEM)] * len(operands),
        out_specs=[pl.BlockSpec(memory_space=pltpu.VMEM)] * outs,
        compiler_params=pltpu.CompilerParams(vmem_limit_bytes=VMEM_LIMIT),
        cost_estimate=cost(shape[0] * shape[1], 32 * shape[0] * shape[1]),
        name=name,
    )(info, *operands)


def rotation_kernel(sign, in_parts, ring, count, info_ref, *refs):
    outs = refs[-7:-5] if in_parts else refs[-6:-5]
    packed, e_high, e_low, t_high, t_low = refs[-5:]
    half, width = packed.shape
    depth = half // 4
    for k, offset in enumerate((0,) + RINGS):
        at = pl.multiple_of(lax.rem(info_ref[ring] + 4 - offset, 4) * depth, depth)
        if count == 1:
            packed[pl.ds(at, depth), :] = refs[0][k * depth : (k + 1) * depth, :]
        else:
            packed[pl.ds(at, depth), :] = refs[k][...]
    rows = lax.broadcasted_iota(i32, (half, half), 0)
    cols = lax.broadcasted_iota(i32, (half, half), 1)
    triangles = packed[:, :half]
    flipped = -triangles.T
    corner = packed[:, half:]

    def put(r, c, value):
        if sign < 0:
            value = -value
        high, low = split(value)
        e_high[r * half : (r + 1) * half, c * half : (c + 1) * half] = high
        e_low[r * half : (r + 1) * half, c * half : (c + 1) * half] = low

    put(0, 0, jnp.where(rows < cols, triangles, flipped))
    put(1, 1, jnp.where(rows > cols, triangles, flipped))
    put(0, 1, corner)
    put(1, 0, -corner.T)
    tile = 256

    for n in range(width // tile):
        lo, hi = n * tile, (n + 1) * tile
        square = 0.5 * dot3(e_high[:hi, :], e_low[:hi, :], e_high[:, lo:hi], e_low[:, lo:hi])
        t_high[:hi, lo:hi], t_low[:hi, lo:hi] = split(square)
        if n > 0:
            t_high[lo:hi, :lo], t_low[lo:hi, :lo] = split(square[:lo].T)

    def store(r0, r1, c0, c1, value):
        if in_parts:
            outs[0][r0:r1, c0:c1], outs[1][r0:r1, c0:c1] = split(value)
        else:
            outs[0][r0:r1, c0:c1] = value

    for n in range(width // tile):
        lo, hi = n * tile, (n + 1) * tile
        odd = dot3(e_high[:hi, :], e_low[:hi, :], t_high[:, lo:hi], t_low[:, lo:hi])
        odd = odd + (e_high[:hi, lo:hi].astype(f32) + e_low[:hi, lo:hi].astype(f32))
        even = t_high[:hi, lo:hi].astype(f32) + t_low[:hi, lo:hi].astype(f32)
        here = lax.broadcasted_iota(i32, (hi, tile), 0)
        there = lax.broadcasted_iota(i32, (hi, tile), 1) + lo
        store(0, hi, lo, hi, even + odd + jnp.where(here == there, 1.0, 0.0))
        if n > 0:
            store(lo, hi, 0, lo, (even[:lo] - odd[:lo]).T)


def rotation(info, pieces, ring, sign, in_parts, after, name):
    width = pieces[0].shape[1]
    square = (width, width)
    if in_parts:
        shapes = [jax.ShapeDtypeStruct(square, bf16)] * 2
    else:
        shapes = [jax.ShapeDtypeStruct(square, f32)]
    return pl.pallas_call(
        functools.partial(rotation_kernel, sign, in_parts, ring, len(pieces)),
        out_shape=shapes,
        in_specs=[pl.BlockSpec(memory_space=pltpu.SMEM)]
        + [pl.BlockSpec(memory_space=pltpu.VMEM)] * len(pieces)
        + [pl.BlockSpec(memory_space=pl.ANY)] * len(after),
        out_specs=[pl.BlockSpec(memory_space=pltpu.VMEM)] * len(shapes),
        scratch_shapes=[pltpu.VMEM((width // 2, width), f32)] + [pltpu.VMEM(square, bf16)] * 4,
        compiler_params=pltpu.CompilerParams(vmem_limit_bytes=5 * VMEM_LIMIT // 4),
        cost_estimate=cost(12 * width**3, 6 * width * width),
        name=name,
    )(info, *pieces, *after)


def right_kernel(jobs, info_ref, m_ref, high_ref, low_ref, *refs):
    width = high_ref.shape[0]
    half = width // 2
    for (slots, which), out_ref in zip(jobs, refs[-len(jobs) :]):
        cols = pl.ds(pl.multiple_of(info_ref[which] * half, half), half)
        for k, slot in enumerate(slots):
            rows = pl.ds(pl.multiple_of(info_ref[slot] * width, width), width)
            m_high, m_low = split(m_ref[rows, :])
            out_ref[k * width : (k + 1) * width, :] = dot3(
                m_high, m_low, high_ref[:, cols], low_ref[:, cols]
            )


def right(info, jobs, matrix, r_high, r_low, after, name):
    width = matrix.shape[1]
    half = width // 2
    return pl.pallas_call(
        functools.partial(right_kernel, jobs),
        out_shape=[jax.ShapeDtypeStruct((len(slots) * width, half), f32) for slots, _ in jobs],
        in_specs=[pl.BlockSpec(memory_space=pltpu.SMEM)]
        + [pl.BlockSpec(memory_space=pltpu.VMEM)] * 3
        + [pl.BlockSpec(memory_space=pl.ANY)] * len(after),
        out_specs=[pl.BlockSpec(memory_space=pltpu.VMEM)] * len(jobs),
        compiler_params=pltpu.CompilerParams(vmem_limit_bytes=VMEM_LIMIT),
        cost_estimate=cost(9 * width**3, 8 * width * width),
        name=name,
    )(info, matrix, r_high, r_low, *after)


def left_product(info_ref, rows, turned_ref, part_refs):
    half = turned_ref.shape[0] // 2
    at = pl.ds(pl.multiple_of(info_ref[rows] * half, half), half)
    part = part_refs[0][...]
    if len(part_refs) > 1:
        part = jnp.where(info_ref[END_COL] > 0, part_refs[1][...], part)
    return dot3(*split(turned_ref[at, :]), *split(part))


def left_kernel(rows, count, info_ref, turned_ref, *refs):
    refs[-1][...] = left_product(info_ref, rows, turned_ref, refs[:count])


def left(info, rows, turned, part, after, name):
    width = turned.shape[0]
    half = width // 2
    in_specs = [pl.BlockSpec(memory_space=pltpu.SMEM)]
    in_specs += [pl.BlockSpec(memory_space=pltpu.VMEM)] * (1 + len(part))
    in_specs += [pl.BlockSpec(memory_space=pl.ANY)] * len(after)
    return pl.pallas_call(
        functools.partial(left_kernel, rows, len(part)),
        out_shape=jax.ShapeDtypeStruct((half, half), f32),
        in_specs=in_specs,
        out_specs=pl.BlockSpec(memory_space=pltpu.VMEM),
        compiler_params=pltpu.CompilerParams(vmem_limit_bytes=VMEM_LIMIT),
        cost_estimate=cost(3 * width**3 // 2, 6 * width * width, LEFT_SHARE),
        name=name,
    )(info, turned, *part, *after)


def keep_kernel(jobs, info_ref, *refs):
    out_ref, kept, sems = refs[-3:]
    half = kept.shape[1]
    copies = []
    for k, (rows, turned, part, row, block) in enumerate(jobs):
        kept[k] = left_product(info_ref, rows, refs[turned], [refs[p] for p in part])
        out_rows = pl.ds(pl.multiple_of(info_ref[row] * half, half), half)
        out_cols = pl.ds(pl.multiple_of(info_ref[block] * half, half), half)
        copy = pltpu.make_async_copy(kept.at[k], out_ref.at[out_rows, out_cols], sems.at[k])
        copy.start()
        copies.append(copy)
    for copy in copies:
        copy.wait()


def keep(info, jobs, operands, after, shape):
    half = operands[0].shape[0] // 2
    in_specs = [pl.BlockSpec(memory_space=pltpu.SMEM)]
    in_specs += [pl.BlockSpec(memory_space=pltpu.VMEM)] * len(operands)
    in_specs += [pl.BlockSpec(memory_space=pl.ANY)] * len(after)
    return pl.pallas_call(
        functools.partial(keep_kernel, jobs),
        out_shape=jax.ShapeDtypeStruct(shape, f32),
        in_specs=in_specs,
        out_specs=pl.BlockSpec(memory_space=pl.ANY),
        scratch_shapes=[
            pltpu.VMEM((len(jobs), half, half), f32),
            pltpu.SemaphoreType.DMA((len(jobs),)),
        ],
        compiler_params=pltpu.CompilerParams(vmem_limit_bytes=VMEM_LIMIT),
        cost_estimate=cost(48 * half**3, 48 * half * half, LEFT_SHARE),
        name="keep",
    )(info, *operands, *after)


def land_kernel(end, info_ref, arrived_ref, own_ref, *refs):
    refs[-1][...] = jnp.where(info_ref[end] > 0, own_ref[...], arrived_ref[...])


def land(info, row, block, end, arrived, own, result, name):
    half = arrived.shape[0]
    tile = 256
    per_half = half // tile
    part = pl.BlockSpec((tile, half), lambda i, info: (i, 0))
    operands, in_specs = [arrived, own], [part, part]
    return pl.pallas_call(
        functools.partial(land_kernel, end),
        out_shape=jax.ShapeDtypeStruct(result.shape, f32),
        grid_spec=pltpu.PrefetchScalarGridSpec(
            num_scalar_prefetch=1,
            grid=(per_half,),
            in_specs=in_specs + [pl.BlockSpec(memory_space=pl.ANY)],
            out_specs=pl.BlockSpec(
                (tile, half), lambda i, info: (info[row] * per_half + i, info[block])
            ),
        ),
        input_output_aliases={1 + len(operands): 0},
        compiler_params=pltpu.CompilerParams(vmem_limit_bytes=VMEM_LIMIT),
        cost_estimate=cost(half * half, 12 * half * half),
        name=name,
    )(info, *operands, result)


def late_kernel(info_ref, late_ref, hop_ref, result_ref, out_ref, sems):
    half = hop_ref.shape[0]

    def copy(k, source, row, block):
        rows = pl.ds(pl.multiple_of(info_ref[row] * half, half), half)
        cols = pl.ds(pl.multiple_of(info_ref[block] * half, half), half)
        return pltpu.make_async_copy(source, out_ref.at[rows, cols], sems.at[k])

    @pl.when(info_ref[HAS_LATE] > 0)
    def _():
        near = copy(0, late_ref.at[:half], LAND_FIRST, NEAR_BLOCK)
        far = copy(1, late_ref.at[half:], LAND_FIRST, FAR_BLOCK)
        near.start()
        far.start()
        near.wait()
        far.wait()

    @pl.when(info_ref[HAS_HOP] > 0)
    def _():
        near = copy(2, hop_ref, LAND_SECOND, NEAR_BLOCK)
        near.start()
        near.wait()


def land_late(info, late, hop, result):
    in_vmem = pl.BlockSpec(memory_space=pltpu.VMEM)
    anywhere = pl.BlockSpec(memory_space=pl.ANY)
    return pl.pallas_call(
        late_kernel,
        out_shape=jax.ShapeDtypeStruct(result.shape, f32),
        in_specs=[pl.BlockSpec(memory_space=pltpu.SMEM), in_vmem, in_vmem, anywhere],
        out_specs=anywhere,
        scratch_shapes=[pltpu.SemaphoreType.DMA((3,))],
        input_output_aliases={3: 0},
        compiler_params=pltpu.CompilerParams(vmem_limit_bytes=VMEM_LIMIT),
        cost_estimate=cost(late.size, 16 * late.size),
        name="land_late",
    )(info, late, hop, result)


def group_pairs(group, ring, plane, senders):
    pairs = []
    for row in range(8):
        for col in range(16):
            chip, core = col // 2, col % 2
            if not senders(row, chip):
                continue
            member = row if group == "row" else chip
            member = (member // 4 ^ plane) * 4 + (member + ring) % 4
            target = (member, col) if group == "row" else (row, 2 * member + core)
            pairs.append((row * 16 + col, target[0] * 16 + target[1]))
    return pairs


def is_source(row, chip):
    return row == chip


def in_source_plane(row, chip):
    return row // 4 == chip // 4


def anyone(row, chip):
    return True


def local(matrix):
    row = lax.axis_index("row")
    col = lax.axis_index("col")
    chip = col // 2
    core = col % 2
    rows_here = matrix.shape[0]
    at_end = (col == 0) | (col == 15)
    near_half = jnp.where((core == 1) | (col == 0), 1, 0)
    out_top = jnp.where(row == 0, 0, 1)
    moved_first = jnp.where(core == 0, out_top, 0)
    moved_second = jnp.where(core == 0, 0, out_top)
    values = {
        CORE: core,
        SOURCE: is_source(row, chip),
        SOURCE_PLANE: in_source_plane(row, chip),
        RING_COL: row % 4,
        RING_ROW: chip % 4,
        FAR_FIRST: jnp.where(at_end, core, 1 - core),
        FAR_SECOND: jnp.where(at_end, 1 - core, core),
        FAR_HALF: 1 - near_half,
        NEAR_HALF: near_half,
        NEAR_FIRST: 1 - core,
        NEAR_SECOND: core,
        MOVED_FIRST: moved_first,
        MOVED_SECOND: moved_second,
        STAYS_FIRST: 1 - moved_first,
        STAYS_SECOND: 1 - moved_second,
        KEPT_FIRST: jnp.where(core == 0, 2, 1),
        KEPT_SECOND: jnp.where(core == 0, 1, 2),
        NEAR_BLOCK: 1 - core,
        FAR_BLOCK: core,
        LAND_FIRST: jnp.where(core == 0, 3, 0),
        LAND_SECOND: jnp.where(core == 0, 0, 3),
        END_FIRST: jnp.where(core == 0, row == 7, row == 0),
        END_SECOND: jnp.where(core == 0, row == 0, row == 7),
        END_COL: at_end,
        HAS_LATE: row == 3 + core,
        HAS_HOP: row == 4 - core,
    }
    info = jnp.stack([jnp.asarray(values[k], i32) for k in range(len(values))])

    own, *quarters = pack(info, matrix)
    arrived = [
        lax.ppermute(quarter, AXES, group_pairs(group, ring, 0, is_source))
        for group in AXES
        for ring, quarter in zip(RINGS, quarters)
    ]
    held = list(small(merge_kernel, info, [own] + arrived, 2, "merge"))
    def cross(group, one):
        return lax.ppermute(one, AXES, group_pairs(group, 0, 1, in_source_plane))

    def around(group, one):
        return [one] + [
            lax.ppermute(one, AXES, group_pairs(group, ring, 0, anyone)) for ring in RINGS
        ]

    col_held, row_held = held
    col_own, row_held = small(
        choose_kernel, info, [cross("row", col_held), col_held, row_held], 2, "choose_col"
    )
    col_pieces = around("row", col_own)
    (row_own,) = small(choose_kernel, info, [cross("col", row_held), row_held], 1, "choose_row")
    row_pieces = around("col", row_own)

    swap = [(i, i ^ 1) for i in range(16)]
    chips = [(i, i - 1) for i in range(2, 16, 2)] + [(i, i + 1) for i in range(1, 15, 2)]

    def row_pairs(down_core, middle, others):
        pairs = []
        for r in range(8):
            for c in range(16):
                target = r - 1 if c % 2 == down_core else r + 1
                if 0 <= target < 8 and (middle if {r, target} == {3, 4} else others):
                    pairs.append((r * 16 + c, target * 16 + c))
        return pairs

    def leave(k, turned, part, after):
        rows = (MOVED_FIRST, MOVED_SECOND)[k // 2]
        moved = left(info, rows, turned, part, after, "leave_%d" % k)
        return moved, lax.ppermute(moved, AXES, row_pairs(k // 2, k == 3, True))

    def detour(down_core, first):
        pairs = []
        for c in range(16):
            hops = (4, 0, 3) if c % 2 == down_core else (3, 7, 4)
            sender, target = hops[:2] if first else hops[1:]
            pairs.append((sender * 16 + c, target * 16 + c))
        return pairs

    row_all = jnp.concatenate(row_pieces, axis=0)
    r_high, r_low = rotation(info, col_pieces, RING_COL, 1, True, [row_own], "column_rotation")
    factors = (matrix, r_high, r_low)
    parts = []
    for slot, which, name in (
        (FAR_FIRST, FAR_HALF, "right_far_first"),
        (FAR_SECOND, FAR_HALF, "right_far_second"),
        (NEAR_FIRST, NEAR_HALF, "right_near_first"),
        (NEAR_SECOND, NEAR_HALF, "right_near_second"),
    ):
        after = parts[-1:] if parts else [row_all]
        (sent,) = right(info, [([slot], which)], *factors, after, name)
        parts.append(sent)
    far_first, far_second = ((lax.ppermute(part, "col", chips), part) for part in parts[:2])
    near_first, near_second = ((lax.ppermute(part, "col", swap),) for part in parts[2:])
    (turned,) = rotation(info, [row_all], RING_ROW, -1, False, parts[3:], "row_rotation")
    other_turned = lax.ppermute(turned, "col", swap)
    moved, landing = [None] * 4, [None] * 4
    moved[1], landing[1] = leave(1, turned, far_first, [])
    moved[0], landing[0] = leave(0, turned, near_first, [moved[1]])
    late = stacked(info, moved[0], moved[1], moved[0])
    moved[2], landing[2] = leave(2, other_turned, near_second, [late])
    late = lax.ppermute(late, AXES, row_pairs(0, True, False))
    hop = lax.ppermute(moved[2], AXES, detour(1, True))
    moved[3], landing[3] = leave(3, other_turned, far_second, [moved[2]])
    operands = [turned, other_turned, *near_first, *far_first, *near_second, *far_second]
    jobs = [
        (STAYS_FIRST, 0, (2,), KEPT_FIRST, NEAR_BLOCK),
        (STAYS_FIRST, 0, (3, 4), KEPT_FIRST, FAR_BLOCK),
        (STAYS_SECOND, 1, (5,), KEPT_SECOND, NEAR_BLOCK),
        (STAYS_SECOND, 1, (6, 7), KEPT_SECOND, FAR_BLOCK),
    ]
    result = keep(info, jobs, operands, [moved[3], hop], matrix.shape)
    hop = lax.ppermute(hop, AXES, detour(1, False))
    for k in (1, 0, 2, 3):
        result = land(
            info,
            (LAND_FIRST, LAND_SECOND)[k // 2],
            (NEAR_BLOCK, FAR_BLOCK)[k % 2],
            (END_FIRST, END_SECOND)[k // 2],
            landing[k],
            moved[(k + 2) % 4],
            result,
            "land_%d" % k,
        )
    return land_late(info, late, hop, result)


def solution(mesh):
    return jax.shard_map(
        local, mesh=mesh, in_specs=(P("row", "col"),), out_specs=P("row", "col"), check_vma=False
    )
```

```python
import functools

import jax
import jax.numpy as jnp
from jax import lax
from jax.experimental import pallas as pl
from jax.experimental.pallas import tpu as pltpu
from jax.sharding import PartitionSpec as P

f32, bf16, i32 = jnp.float32, jnp.bfloat16, jnp.int32
AXES = ("row", "col")
VMEM_LIMIT = 16 * 1024 * 1024


def cost(flops, nbytes, share=1 / 64):
    return pl.CostEstimate(
        flops=int(flops * share), bytes_accessed=int(nbytes * share), transcendentals=0
    )


LEFT_SHARE = 16


def split(value):
    high = value.astype(bf16)
    return high, (value - high.astype(f32)).astype(bf16)


def dot(a, b):
    return jnp.dot(a, b, preferred_element_type=f32)


def dot3(a_high, a_low, b_high, b_low):
    return dot(a_high, b_high) + (dot(a_high, b_low) + dot(a_low, b_high))


CORE, SOURCE, SOURCE_PLANE, RING_COL, RING_ROW = range(5)
FAR_FIRST, FAR_SECOND, FAR_HALF, NEAR_HALF, NEAR_FIRST, NEAR_SECOND = range(5, 11)
MOVED_FIRST, MOVED_SECOND, STAYS_FIRST, STAYS_SECOND = range(11, 15)
KEPT_FIRST, KEPT_SECOND, NEAR_BLOCK, FAR_BLOCK = range(15, 19)
LAND_FIRST, LAND_SECOND, END_FIRST, END_SECOND, END_COL = range(19, 24)
HAS_LATE, HAS_HOP = range(24, 26)
RINGS = (1, 3, 2)


def pack_kernel(info_ref, block_ref, *refs):
    out_refs, packed = refs[:4], refs[4]
    width = block_ref.shape[0]
    half = width // 2
    rows = lax.broadcasted_iota(i32, (half, half), 0)
    cols = lax.broadcasted_iota(i32, (half, half), 1)
    on_diagonal = rows == cols
    top = block_ref[:half, :half]
    bottom = block_ref[half:, half:]
    top_only = jnp.where(on_diagonal, top, 0.0)
    bottom_only = jnp.where(on_diagonal, bottom, 0.0)
    top_down = jnp.sum(top_only, axis=1, keepdims=True)
    top_across = jnp.sum(top_only, axis=0, keepdims=True)
    bottom_down = jnp.sum(bottom_only, axis=1, keepdims=True)
    bottom_across = jnp.sum(bottom_only, axis=0, keepdims=True)
    above = rows < cols
    value = jnp.where(above, top, bottom)
    spacing = jnp.where(above, top_across - top_down, bottom_across - bottom_down)
    packed[:, :half] = jnp.where(
        on_diagonal, 0.0, value / jnp.where(on_diagonal, 1.0, spacing)
    )
    packed[:, half:] = block_ref[:half, half:] / (bottom_across - top_down)
    depth = half // 4
    for out_ref, ring in zip(out_refs, (0,) + RINGS):
        at = pl.multiple_of(lax.rem(info_ref[RING_COL] + ring, 4) * depth, depth)
        out_ref[...] = packed[pl.ds(at, depth), :]


def pack(info, matrix):
    width = matrix.shape[1]
    half = width // 2
    out = jax.ShapeDtypeStruct((half // 4, width), f32)
    out_spec = pl.BlockSpec((half // 4, width), lambda i, info: (0, 0))
    return pl.pallas_call(
        pack_kernel,
        out_shape=[out] * 4,
        grid_spec=pltpu.PrefetchScalarGridSpec(
            num_scalar_prefetch=1,
            grid=(1,),
            in_specs=[pl.BlockSpec((width, width), lambda i, info: (info[CORE], 0))],
            out_specs=[out_spec] * 4,
            scratch_shapes=[pltpu.VMEM((half, width), f32)],
        ),
        compiler_params=pltpu.CompilerParams(vmem_limit_bytes=VMEM_LIMIT),
        cost_estimate=cost(8 * width * width, 6 * width * width),
        name="pack",
    )(info, matrix)


def merge_kernel(info_ref, own, *refs):
    for group in range(2):
        arrived = refs[3 * group : 3 * group + 3]
        total = arrived[0][...] + arrived[1][...] + arrived[2][...]
        refs[6 + group][...] = jnp.where(info_ref[SOURCE] > 0, own[...], total)


def choose_kernel(info_ref, across, held, *refs):
    outs = refs[len(refs) // 2 :]
    outs[0][...] = jnp.where(info_ref[SOURCE_PLANE] > 0, held[...], across[...])
    if len(refs) > 1:
        outs[1][...] = refs[0][...]


def stack_kernel(info_ref, top, bottom, after, out):
    rows = top.shape[0]
    out[:rows, :] = top[...]
    out[rows:, :] = bottom[...]


def stacked(info, top, bottom, after):
    rows, width = top.shape
    return pl.pallas_call(
        stack_kernel,
        out_shape=jax.ShapeDtypeStruct((2 * rows, width), f32),
        in_specs=[pl.BlockSpec(memory_space=pltpu.SMEM)]
        + [pl.BlockSpec(memory_space=pltpu.VMEM)] * 2
        + [pl.BlockSpec(memory_space=pl.ANY)],
        out_specs=pl.BlockSpec(memory_space=pltpu.VMEM),
        compiler_params=pltpu.CompilerParams(vmem_limit_bytes=VMEM_LIMIT),
        cost_estimate=cost(rows * width, 16 * rows * width),
        name="stacked",
    )(info, top, bottom, after)


def small(kernel, info, operands, outs, name):
    shape = operands[0].shape
    return pl.pallas_call(
        kernel,
        out_shape=[jax.ShapeDtypeStruct(shape, f32)] * outs,
        in_specs=[pl.BlockSpec(memory_space=pltpu.SMEM)]
        + [pl.BlockSpec(memory_space=pltpu.VMEM)] * len(operands),
        out_specs=[pl.BlockSpec(memory_space=pltpu.VMEM)] * outs,
        compiler_params=pltpu.CompilerParams(vmem_limit_bytes=VMEM_LIMIT),
        cost_estimate=cost(shape[0] * shape[1], 32 * shape[0] * shape[1]),
        name=name,
    )(info, *operands)


def rotation_kernel(sign, in_parts, ring, count, info_ref, *refs):
    outs = refs[-7:-5] if in_parts else refs[-6:-5]
    packed, e_high, e_low, t_high, t_low = refs[-5:]
    half, width = packed.shape
    depth = half // 4
    for k, offset in enumerate((0,) + RINGS):
        at = pl.multiple_of(lax.rem(info_ref[ring] + 4 - offset, 4) * depth, depth)
        if count == 1:
            packed[pl.ds(at, depth), :] = refs[0][k * depth : (k + 1) * depth, :]
        else:
            packed[pl.ds(at, depth), :] = refs[k][...]
    rows = lax.broadcasted_iota(i32, (half, half), 0)
    cols = lax.broadcasted_iota(i32, (half, half), 1)
    triangles = packed[:, :half]
    flipped = -triangles.T
    corner = packed[:, half:]

    def put(r, c, value):
        if sign < 0:
            value = -value
        high, low = split(value)
        e_high[r * half : (r + 1) * half, c * half : (c + 1) * half] = high
        e_low[r * half : (r + 1) * half, c * half : (c + 1) * half] = low

    put(0, 0, jnp.where(rows < cols, triangles, flipped))
    put(1, 1, jnp.where(rows > cols, triangles, flipped))
    put(0, 1, corner)
    put(1, 0, -corner.T)
    tile = 256

    for n in range(width // tile):
        lo, hi = n * tile, (n + 1) * tile
        square = 0.5 * dot3(e_high[:hi, :], e_low[:hi, :], e_high[:, lo:hi], e_low[:, lo:hi])
        t_high[:hi, lo:hi], t_low[:hi, lo:hi] = split(square)
        if n > 0:
            t_high[lo:hi, :lo], t_low[lo:hi, :lo] = split(square[:lo].T)

    def store(r0, r1, c0, c1, value):
        if in_parts:
            outs[0][r0:r1, c0:c1], outs[1][r0:r1, c0:c1] = split(value)
        else:
            outs[0][r0:r1, c0:c1] = value

    for n in range(width // tile):
        lo, hi = n * tile, (n + 1) * tile
        odd = dot3(e_high[:hi, :], e_low[:hi, :], t_high[:, lo:hi], t_low[:, lo:hi])
        odd = odd + (e_high[:hi, lo:hi].astype(f32) + e_low[:hi, lo:hi].astype(f32))
        even = t_high[:hi, lo:hi].astype(f32) + t_low[:hi, lo:hi].astype(f32)
        here = lax.broadcasted_iota(i32, (hi, tile), 0)
        there = lax.broadcasted_iota(i32, (hi, tile), 1) + lo
        store(0, hi, lo, hi, even + odd + jnp.where(here == there, 1.0, 0.0))
        if n > 0:
            store(lo, hi, 0, lo, (even[:lo] - odd[:lo]).T)


def rotation(info, pieces, ring, sign, in_parts, after, name):
    width = pieces[0].shape[1]
    square = (width, width)
    if in_parts:
        shapes = [jax.ShapeDtypeStruct(square, bf16)] * 2
    else:
        shapes = [jax.ShapeDtypeStruct(square, f32)]
    return pl.pallas_call(
        functools.partial(rotation_kernel, sign, in_parts, ring, len(pieces)),
        out_shape=shapes,
        in_specs=[pl.BlockSpec(memory_space=pltpu.SMEM)]
        + [pl.BlockSpec(memory_space=pltpu.VMEM)] * len(pieces)
        + [pl.BlockSpec(memory_space=pl.ANY)] * len(after),
        out_specs=[pl.BlockSpec(memory_space=pltpu.VMEM)] * len(shapes),
        scratch_shapes=[pltpu.VMEM((width // 2, width), f32)] + [pltpu.VMEM(square, bf16)] * 4,
        compiler_params=pltpu.CompilerParams(vmem_limit_bytes=5 * VMEM_LIMIT // 4),
        cost_estimate=cost(12 * width**3, 6 * width * width),
        name=name,
    )(info, *pieces, *after)


def right_kernel(jobs, info_ref, m_ref, high_ref, low_ref, *refs):
    width = high_ref.shape[0]
    half = width // 2
    for (slots, which), out_ref in zip(jobs, refs[-len(jobs) :]):
        cols = pl.ds(pl.multiple_of(info_ref[which] * half, half), half)
        for k, slot in enumerate(slots):
            rows = pl.ds(pl.multiple_of(info_ref[slot] * width, width), width)
            m_high, m_low = split(m_ref[rows, :])
            out_ref[k * width : (k + 1) * width, :] = dot3(
                m_high, m_low, high_ref[:, cols], low_ref[:, cols]
            )


def right(info, jobs, matrix, r_high, r_low, after, name):
    width = matrix.shape[1]
    half = width // 2
    return pl.pallas_call(
        functools.partial(right_kernel, jobs),
        out_shape=[jax.ShapeDtypeStruct((len(slots) * width, half), f32) for slots, _ in jobs],
        in_specs=[pl.BlockSpec(memory_space=pltpu.SMEM)]
        + [pl.BlockSpec(memory_space=pltpu.VMEM)] * 3
        + [pl.BlockSpec(memory_space=pl.ANY)] * len(after),
        out_specs=[pl.BlockSpec(memory_space=pltpu.VMEM)] * len(jobs),
        compiler_params=pltpu.CompilerParams(vmem_limit_bytes=VMEM_LIMIT),
        cost_estimate=cost(9 * width**3, 8 * width * width),
        name=name,
    )(info, matrix, r_high, r_low, *after)


def left_product(info_ref, rows, turned_ref, part_refs):
    half = turned_ref.shape[0] // 2
    at = pl.ds(pl.multiple_of(info_ref[rows] * half, half), half)
    part = part_refs[0][...]
    if len(part_refs) > 1:
        part = jnp.where(info_ref[END_COL] > 0, part_refs[1][...], part)
    return dot3(*split(turned_ref[at, :]), *split(part))


def left_kernel(rows, count, info_ref, turned_ref, *refs):
    refs[-1][...] = left_product(info_ref, rows, turned_ref, refs[:count])


def left(info, rows, turned, part, after, name):
    width = turned.shape[0]
    half = width // 2
    in_specs = [pl.BlockSpec(memory_space=pltpu.SMEM)]
    in_specs += [pl.BlockSpec(memory_space=pltpu.VMEM)] * (1 + len(part))
    in_specs += [pl.BlockSpec(memory_space=pl.ANY)] * len(after)
    return pl.pallas_call(
        functools.partial(left_kernel, rows, len(part)),
        out_shape=jax.ShapeDtypeStruct((half, half), f32),
        in_specs=in_specs,
        out_specs=pl.BlockSpec(memory_space=pltpu.VMEM),
        compiler_params=pltpu.CompilerParams(vmem_limit_bytes=VMEM_LIMIT),
        cost_estimate=cost(3 * width**3 // 2, 6 * width * width, LEFT_SHARE),
        name=name,
    )(info, turned, *part, *after)


def keep_kernel(jobs, info_ref, *refs):
    out_ref, kept, sems = refs[-3:]
    half = kept.shape[1]
    copies = []
    for k, (rows, turned, part, row, block) in enumerate(jobs):
        kept[k] = left_product(info_ref, rows, refs[turned], [refs[p] for p in part])
        out_rows = pl.ds(pl.multiple_of(info_ref[row] * half, half), half)
        out_cols = pl.ds(pl.multiple_of(info_ref[block] * half, half), half)
        copy = pltpu.make_async_copy(kept.at[k], out_ref.at[out_rows, out_cols], sems.at[k])
        copy.start()
        copies.append(copy)
    for copy in copies:
        copy.wait()


def keep(info, jobs, operands, after, shape):
    half = operands[0].shape[0] // 2
    in_specs = [pl.BlockSpec(memory_space=pltpu.SMEM)]
    in_specs += [pl.BlockSpec(memory_space=pltpu.VMEM)] * len(operands)
    in_specs += [pl.BlockSpec(memory_space=pl.ANY)] * len(after)
    return pl.pallas_call(
        functools.partial(keep_kernel, jobs),
        out_shape=jax.ShapeDtypeStruct(shape, f32),
        in_specs=in_specs,
        out_specs=pl.BlockSpec(memory_space=pl.ANY),
        scratch_shapes=[
            pltpu.VMEM((len(jobs), half, half), f32),
            pltpu.SemaphoreType.DMA((len(jobs),)),
        ],
        compiler_params=pltpu.CompilerParams(vmem_limit_bytes=VMEM_LIMIT),
        cost_estimate=cost(48 * half**3, 48 * half * half, LEFT_SHARE),
        name="keep",
    )(info, *operands, *after)


def land_kernel(end, info_ref, arrived_ref, own_ref, *refs):
    refs[-1][...] = jnp.where(info_ref[end] > 0, own_ref[...], arrived_ref[...])


def land(info, row, block, end, arrived, own, result, name):
    half = arrived.shape[0]
    tile = 256
    per_half = half // tile
    part = pl.BlockSpec((tile, half), lambda i, info: (i, 0))
    operands, in_specs = [arrived, own], [part, part]
    return pl.pallas_call(
        functools.partial(land_kernel, end),
        out_shape=jax.ShapeDtypeStruct(result.shape, f32),
        grid_spec=pltpu.PrefetchScalarGridSpec(
            num_scalar_prefetch=1,
            grid=(per_half,),
            in_specs=in_specs + [pl.BlockSpec(memory_space=pl.ANY)],
            out_specs=pl.BlockSpec(
                (tile, half), lambda i, info: (info[row] * per_half + i, info[block])
            ),
        ),
        input_output_aliases={1 + len(operands): 0},
        compiler_params=pltpu.CompilerParams(vmem_limit_bytes=VMEM_LIMIT),
        cost_estimate=cost(half * half, 12 * half * half),
        name=name,
    )(info, *operands, result)


def late_kernel(info_ref, late_ref, hop_ref, result_ref, out_ref, sems):
    half = hop_ref.shape[0]

    def copy(k, source, row, block):
        rows = pl.ds(pl.multiple_of(info_ref[row] * half, half), half)
        cols = pl.ds(pl.multiple_of(info_ref[block] * half, half), half)
        return pltpu.make_async_copy(source, out_ref.at[rows, cols], sems.at[k])

    @pl.when(info_ref[HAS_LATE] > 0)
    def _():
        near = copy(0, late_ref.at[:half], LAND_FIRST, NEAR_BLOCK)
        far = copy(1, late_ref.at[half:], LAND_FIRST, FAR_BLOCK)
        near.start()
        far.start()
        near.wait()
        far.wait()

    @pl.when(info_ref[HAS_HOP] > 0)
    def _():
        near = copy(2, hop_ref, LAND_SECOND, NEAR_BLOCK)
        near.start()
        near.wait()


def land_late(info, late, hop, result):
    in_vmem = pl.BlockSpec(memory_space=pltpu.VMEM)
    anywhere = pl.BlockSpec(memory_space=pl.ANY)
    return pl.pallas_call(
        late_kernel,
        out_shape=jax.ShapeDtypeStruct(result.shape, f32),
        in_specs=[pl.BlockSpec(memory_space=pltpu.SMEM), in_vmem, in_vmem, anywhere],
        out_specs=anywhere,
        scratch_shapes=[pltpu.SemaphoreType.DMA((3,))],
        input_output_aliases={3: 0},
        compiler_params=pltpu.CompilerParams(vmem_limit_bytes=VMEM_LIMIT),
        cost_estimate=cost(late.size, 16 * late.size),
        name="land_late",
    )(info, late, hop, result)


def group_pairs(group, ring, plane, senders):
    pairs = []
    for row in range(8):
        for col in range(16):
            chip, core = col // 2, col % 2
            if not senders(row, chip):
                continue
            member = row if group == "row" else chip
            member = (member // 4 ^ plane) * 4 + (member + ring) % 4
            target = (member, col) if group == "row" else (row, 2 * member + core)
            pairs.append((row * 16 + col, target[0] * 16 + target[1]))
    return pairs


def is_source(row, chip):
    return row == chip


def in_source_plane(row, chip):
    return row // 4 == chip // 4


def anyone(row, chip):
    return True


def local(matrix):
    row = lax.axis_index("row")
    col = lax.axis_index("col")
    chip = col // 2
    core = col % 2
    rows_here = matrix.shape[0]
    at_end = (col == 0) | (col == 15)
    near_half = jnp.where((core == 1) | (col == 0), 1, 0)
    out_top = jnp.where(row == 0, 0, 1)
    moved_first = jnp.where(core == 0, out_top, 0)
    moved_second = jnp.where(core == 0, 0, out_top)
    values = {
        CORE: core,
        SOURCE: is_source(row, chip),
        SOURCE_PLANE: in_source_plane(row, chip),
        RING_COL: row % 4,
        RING_ROW: chip % 4,
        FAR_FIRST: jnp.where(at_end, core, 1 - core),
        FAR_SECOND: jnp.where(at_end, 1 - core, core),
        FAR_HALF: 1 - near_half,
        NEAR_HALF: near_half,
        NEAR_FIRST: 1 - core,
        NEAR_SECOND: core,
        MOVED_FIRST: moved_first,
        MOVED_SECOND: moved_second,
        STAYS_FIRST: 1 - moved_first,
        STAYS_SECOND: 1 - moved_second,
        KEPT_FIRST: jnp.where(core == 0, 2, 1),
        KEPT_SECOND: jnp.where(core == 0, 1, 2),
        NEAR_BLOCK: 1 - core,
        FAR_BLOCK: core,
        LAND_FIRST: jnp.where(core == 0, 3, 0),
        LAND_SECOND: jnp.where(core == 0, 0, 3),
        END_FIRST: jnp.where(core == 0, row == 7, row == 0),
        END_SECOND: jnp.where(core == 0, row == 0, row == 7),
        END_COL: at_end,
        HAS_LATE: row == 3 + core,
        HAS_HOP: row == 4 - core,
    }
    info = jnp.stack([jnp.asarray(values[k], i32) for k in range(len(values))])

    own, *quarters = pack(info, matrix)
    arrived = [
        lax.ppermute(quarter, AXES, group_pairs(group, ring, 0, is_source))
        for group in AXES
        for ring, quarter in zip(RINGS, quarters)
    ]
    held = list(small(merge_kernel, info, [own] + arrived, 2, "merge"))
    def cross(group, one):
        return lax.ppermute(one, AXES, group_pairs(group, 0, 1, in_source_plane))

    def around(group, one):
        return [one] + [
            lax.ppermute(one, AXES, group_pairs(group, ring, 0, anyone)) for ring in RINGS
        ]

    col_held, row_held = held
    col_own, row_held = small(
        choose_kernel, info, [cross("row", col_held), col_held, row_held], 2, "choose_col"
    )
    col_pieces = around("row", col_own)
    (row_own,) = small(choose_kernel, info, [cross("col", row_held), row_held], 1, "choose_row")
    row_pieces = around("col", row_own)

    swap = [(i, i ^ 1) for i in range(16)]
    chips = [(i, i - 1) for i in range(2, 16, 2)] + [(i, i + 1) for i in range(1, 15, 2)]

    def row_pairs(down_core, middle, others):
        pairs = []
        for r in range(8):
            for c in range(16):
                target = r - 1 if c % 2 == down_core else r + 1
                if 0 <= target < 8 and (middle if {r, target} == {3, 4} else others):
                    pairs.append((r * 16 + c, target * 16 + c))
        return pairs

    def leave(k, turned, part, after):
        rows = (MOVED_FIRST, MOVED_SECOND)[k // 2]
        moved = left(info, rows, turned, part, after, "leave_%d" % k)
        return moved, lax.ppermute(moved, AXES, row_pairs(k // 2, k == 3, True))

    def detour(down_core, first):
        pairs = []
        for c in range(16):
            hops = (4, 0, 3) if c % 2 == down_core else (3, 7, 4)
            sender, target = hops[:2] if first else hops[1:]
            pairs.append((sender * 16 + c, target * 16 + c))
        return pairs

    row_all = jnp.concatenate(row_pieces, axis=0)
    r_high, r_low = rotation(info, col_pieces, RING_COL, 1, True, [row_own], "column_rotation")
    factors = (matrix, r_high, r_low)
    parts = []
    for slot, which, name in (
        (FAR_FIRST, FAR_HALF, "right_far_first"),
        (FAR_SECOND, FAR_HALF, "right_far_second"),
        (NEAR_FIRST, NEAR_HALF, "right_near_first"),
    ):
        after = parts[-1:] if parts else [row_all]
        (sent,) = right(info, [([slot], which)], *factors, after, name)
        parts.append(sent)
    far_first, far_second = ((lax.ppermute(part, "col", chips), part) for part in parts[:2])
    near_first = (lax.ppermute(parts[2], "col", swap),)
    (turned,) = rotation(info, [row_all], RING_ROW, -1, False, parts[2:], "row_rotation")
    jobs = [([NEAR_SECOND], NEAR_HALF)]
    (sent,) = right(info, jobs, *factors, [turned], "right_near_second")
    near_second = (lax.ppermute(sent, "col", swap),)
    other_turned = lax.ppermute(turned, "col", swap)
    moved, landing = [None] * 4, [None] * 4
    moved[1], landing[1] = leave(1, turned, far_first, [sent])
    moved[0], landing[0] = leave(0, turned, near_first, [moved[1]])
    late = stacked(info, moved[0], moved[1], moved[0])
    moved[2], landing[2] = leave(2, other_turned, near_second, [late])
    late = lax.ppermute(late, AXES, row_pairs(0, True, False))
    hop = lax.ppermute(moved[2], AXES, detour(1, True))
    moved[3], landing[3] = leave(3, other_turned, far_second, [moved[2]])
    operands = [turned, other_turned, *near_first, *far_first, *near_second, *far_second]
    jobs = [
        (STAYS_FIRST, 0, (2,), KEPT_FIRST, NEAR_BLOCK),
        (STAYS_FIRST, 0, (3, 4), KEPT_FIRST, FAR_BLOCK),
        (STAYS_SECOND, 1, (5,), KEPT_SECOND, NEAR_BLOCK),
        (STAYS_SECOND, 1, (6, 7), KEPT_SECOND, FAR_BLOCK),
    ]
    result = keep(info, jobs, operands, [moved[3], hop], matrix.shape)
    hop = lax.ppermute(hop, AXES, detour(1, False))
    for k in (1, 0, 2, 3):
        result = land(
            info,
            (LAND_FIRST, LAND_SECOND)[k // 2],
            (NEAR_BLOCK, FAR_BLOCK)[k % 2],
            (END_FIRST, END_SECOND)[k // 2],
            landing[k],
            moved[(k + 2) % 4],
            result,
            "land_%d" % k,
        )
    return land_late(info, late, hop, result)


def solution(mesh):
    return jax.shard_map(
        local, mesh=mesh, in_specs=(P("row", "col"),), out_specs=P("row", "col"), check_vma=False
    )
```
